768 devices in a mesh: dp: 64 (over y, x, core), mp: 12 (over z).
Axes of the slice: x: 4, y: 8, z: 12, core: 2. Of those that a mesh axis runs over, the one named last changes fastest.
Arguments:
- momentum: float32 [64, 768, 4096], P('dp', 'mp')
- grad: bfloat16 [64, 768, 4096], P('dp', 'mp')
- weights: float32 [768, 4096], P('mp'), may hold values from -6 to 6
- picks: int32 [64, 12, 64, 4], P('dp', 'mp'), may hold values from 0 to 255, as said below
- counts: int32 [64, 12, 64], P('dp', 'mp'), may hold values from 1 to 4, as said below
Outputs:
- new_momentum: float32 [64, 768, 4096], P('dp', 'mp')
- new_weights: float32 [768, 4096], P('mp')
The draws below stay inside these ranges and needn't reach their ends.
Inputs may be any that keep to these rules, and one draw needn't show every extreme that they name: `picks`: for each replica and group, all 4 entries are distinct block numbers. `counts`: every group has some replica with a count of 4.
All inputs are finite; a program needn't handle non-finite values.
Results may differ from the reference program's by a relative error of at most 0.0004.
Values sent between devices are 32-bit elements; how exact they have to be, the bound alone decides.
No kernel may reach another device: no remote copies, remote signals or barrier semaphores. Data moves between devices by JAX's collectives and lax.ppermute only.
A program may use at most 64 MiB of HBM per device.

```python
import jax
import jax.numpy as jnp
from jax import lax

GROUP = 64
BLOCK = 4
KMAX = 4
COLS = 4096
NROWS = 768
N_DP = 64
N_MP = 12


def scaled_field(key, rise):
    row_key, col_key, base_key = jax.random.split(key, 3)
    rows = jnp.arange(NROWS, dtype=jnp.float32)
    lift = rise ** (rows / max(NROWS - 1, 1))
    row_scale = lift * jnp.exp(jax.random.uniform(row_key, (NROWS,), jnp.float32, jnp.log(0.3), jnp.log(3.0)))
    col_scale = jnp.exp(jax.random.uniform(col_key, (COLS,), jnp.float32, jnp.log(0.3), jnp.log(3.0)))
    base = jax.random.normal(base_key, (N_DP, NROWS, COLS), jnp.float32)
    return base * row_scale[None, :, None] * col_scale[None, None, :]


def draw_momentum(key, part):
    key = jax.random.fold_in(key, 11)
    return scaled_field(key, 3.0)


def draw_grad(key, part):
    key = jax.random.fold_in(key, 12)
    return scaled_field(key, 3.0).astype(jnp.bfloat16)


def draw_picks(key, part):
    key = jax.random.fold_in(key, 13)
    blocks_all = (GROUP // BLOCK) ** 2
    scores = jax.random.randint(key, (N_DP, N_MP, COLS // GROUP, blocks_all), 0, 1 << 20)
    scores = scores * blocks_all + jnp.arange(blocks_all, dtype=jnp.int32)
    chosen = lax.top_k(scores, KMAX)[1]
    return chosen.astype(jnp.int32)


def draw_counts(key, part):
    key = jax.random.fold_in(key, 14)
    base_key, owner_key = jax.random.split(key)
    base = jax.random.randint(base_key, (N_DP, N_MP, COLS // GROUP), 1, KMAX + 1)
    owner = jax.random.randint(owner_key, (N_MP, COLS // GROUP), 0, N_DP)
    replica = jnp.arange(N_DP, dtype=jnp.int32)[:, None, None]
    return jnp.where(replica == owner[None], KMAX, base).astype(jnp.int32)


def block_levels(key, extent, cuts, low, largest):
    factor_of, own = 1.0, jax.random.fold_in(key, 6)
    for position, shards_of in cuts:
        steps = jnp.exp(jax.random.uniform(jax.random.fold_in(own, position), (shards_of,), jnp.float32, low / len(cuts), largest / len(cuts)))
        factor_of = factor_of * jnp.repeat(steps, extent[position] // shards_of).reshape([-1 if axis == position else 1 for axis in range(len(extent))])
    return factor_of


def scatter_about(key, extent, scale, limit, cuts=(), held_as=jnp.bfloat16):
    drawn = scale * jax.random.normal(key, extent, jnp.float32)
    if cuts:
        drawn = drawn * block_levels(key, extent, cuts, -0.22, 0.18)
    return jnp.clip(drawn, -limit, limit).astype(held_as)


def setup_inputs(seed: int = 0) -> dict:
    key_of = jax.random.split(jax.random.key(seed), 6)
    momentum = draw_momentum(jax.random.fold_in(key_of[5], 71), 0)
    grad = draw_grad(jax.random.fold_in(key_of[5], 71), 0)
    weights = scatter_about(key_of[2], (NROWS, COLS), 1.0, 6.0, ((0, 12),), jnp.float32)
    picks = draw_picks(jax.random.fold_in(key_of[5], 71), 0)
    counts = draw_counts(jax.random.fold_in(key_of[5], 71), 0)
    return {"momentum": momentum, "grad": grad, "weights": weights, "picks": picks, "counts": counts}


def basis(size):
    rows = jnp.arange(size, dtype=jnp.float32)[:, None]
    cols = jnp.arange(size, dtype=jnp.float32)[None, :]
    waves = jnp.cos(jnp.pi * (2.0 * cols + 1.0) * rows / (2.0 * size))
    factor = jnp.where(rows == 0.0, jnp.sqrt(1.0 / size), jnp.sqrt(2.0 / size))
    return (waves * factor).astype(jnp.float32)

def forward_groups(bas, field):
    groups = field.reshape(N_MP, GROUP, COLS // GROUP, GROUP)
    left = jnp.einsum('uk,rkcn->rcun', bas, groups, precision=lax.Precision.HIGHEST)
    return jnp.einsum('rcun,vn->rcuv', left, bas, precision=lax.Precision.HIGHEST)

def inverse_groups(bas, coef):
    left = jnp.einsum('uk,rcuv->rckv', bas, coef, precision=lax.Precision.HIGHEST)
    back = jnp.einsum('rckv,vn->rkcn', left, bas, precision=lax.Precision.HIGHEST)
    return back.reshape(N_MP * GROUP, COLS)

def reference(momentum, grad, weights, picks, counts):
    bas = basis(GROUP)
    side = GROUP // BLOCK
    blocks_all = side * side
    nchunk = COLS // GROUP

    def one(total, items):
        moment_in, grad_in, picked, counted = items
        moment = 0.9 * moment_in + grad_in.astype(jnp.float32)
        coef = forward_groups(bas, moment)
        valid = jnp.arange(KMAX, dtype=jnp.int32)[None, None, :] < counted[:, :, None]
        hits = (picked[..., None] == jnp.arange(blocks_all, dtype=jnp.int32)) & valid[..., None]
        mask = jnp.any(hits, axis=2).astype(jnp.float32).reshape(N_MP, nchunk, side, 1, side, 1)
        kept = (coef.reshape(N_MP, nchunk, side, BLOCK, side, BLOCK) * mask).reshape(N_MP, nchunk, GROUP, GROUP)
        return (total + kept, moment - inverse_groups(bas, kept))
    start = jnp.zeros((N_MP, nchunk, GROUP, GROUP), jnp.float32)
    total, new_momentum = lax.scan(one, start, (momentum, grad, picks, counts))
    avg = total / N_DP
    update = inverse_groups(bas, avg)
    scale = jnp.sqrt(jnp.mean(update * update) + 1e-06)
    new_weights = weights - 0.5 * update / scale
    return (new_momentum, new_weights)
```

```python
import functools

import jax
import jax.numpy as jnp
import ml_dtypes
import numpy as np
from jax import lax
from jax.experimental import pallas as pl
from jax.experimental.pallas import tpu as pltpu
from jax.sharding import PartitionSpec as P

GROUP = 64
BLOCK = 4
KMAX = 4
SIDE = GROUP // BLOCK
QUAD = 4 * GROUP
ROWS = 40
F32 = jnp.float32
BF16 = jnp.bfloat16
PARAMS = pltpu.CompilerParams(vmem_limit_bytes=48 * 1024 * 1024)


def basis():
    rows = np.arange(GROUP, dtype=np.float64)[:, None]
    cols = np.arange(GROUP, dtype=np.float64)[None, :]
    waves = np.cos(np.pi * (2.0 * cols + 1.0) * rows / (2.0 * GROUP))
    factor = np.where(rows == 0.0, np.sqrt(1.0 / GROUP), np.sqrt(2.0 / GROUP))
    return (waves * factor).astype(np.float32)


def halves(mat):
    high = mat.astype(ml_dtypes.bfloat16)
    low = (mat - high.astype(np.float32)).astype(ml_dtypes.bfloat16)
    return high, low


def left_weights(mat):
    high, low = halves(mat)
    return np.concatenate([high, high, low, low], axis=1)


def right_weights(mat):
    return np.stack(halves(np.kron(np.eye(4, dtype=np.float32), mat)))


def scatter_weights(mat):
    perm = np.arange(GROUP).reshape(SIDE, BLOCK).T.reshape(-1)
    return right_weights(mat[perm])


def pack_weights():
    out = np.zeros((4, SIDE, BLOCK, 8, BLOCK, BLOCK), np.float32)
    for group in range(8):
        for col in range(BLOCK):
            out[group % 4, :, col, group, col, :] = 1.0
    return out.reshape(QUAD, 128).astype(ml_dtypes.bfloat16)


def pack_rows():
    out = np.zeros((2, KMAX, 4, KMAX, 2, BLOCK), np.float32)
    for quad in range(4):
        for slot in range(KMAX):
            out[quad // 2, slot, quad, slot] = 1.0
    return np.tile(out.reshape(8, 128), (1, 3)).astype(ml_dtypes.bfloat16)


def iota(shape, axis):
    return lax.broadcasted_iota(jnp.int32, shape, axis)


def dot(a, b):
    return jnp.dot(a, b, preferred_element_type=F32)


def split(x):
    high = x.astype(BF16)
    return high, (x - high.astype(F32)).astype(BF16)


def times_left(weights, x):
    high, low = split(x)
    return dot(weights, jnp.concatenate([high, low, high, low], axis=0))


def times_right(x, weights_ref):
    high, low = split(x)
    top = weights_ref[0]
    return dot(high, top) + (dot(low, top) + dot(high, weights_ref[1]))


def stack_quads(x):
    return jnp.concatenate([x[:, q * QUAD : (q + 1) * QUAD] for q in range(x.shape[1] // QUAD)], axis=0)


def send_kernel(mom_ref, grad_ref, picks_ref, counts_ref, left_ref, right_ref, pack_ref, fold_ref,
                send_ref, kept_ref, moment_ref):
    step = pl.program_id(0)
    width = mom_ref.shape[1]
    quads = width // QUAD
    moment = 0.9 * mom_ref[...] + grad_ref[...].astype(F32)
    moment_ref[...] = moment
    coef = times_right(stack_quads(times_left(left_ref[...], moment)), right_ref)
    valid = iota(picks_ref.shape, 0) < counts_ref[...]
    picks = jnp.where(valid, picks_ref[...].astype(F32), -1.0)
    groups = picks.shape[1]
    picks8 = jnp.concatenate([picks, jnp.full_like(picks, -1.0)], axis=0)
    spread = iota((groups, width), 0) == step * (width // GROUP) + iota((groups, width), 1) // GROUP
    wide = dot(picks8.astype(BF16), jnp.where(spread, 1.0, 0.0).astype(BF16))
    number = (iota((GROUP, QUAD), 0) // BLOCK) * SIDE + (iota((GROUP, QUAD), 1) % GROUP) // BLOCK
    number = number.astype(F32)
    parts = []
    for q in range(quads):
        quad = coef[q * GROUP : (q + 1) * GROUP]
        total = jnp.zeros_like(quad)
        for k in range(KMAX):
            hit = number == wide[k : k + 1, q * QUAD : (q + 1) * QUAD]
            chosen = jnp.where(hit, quad, 0.0)
            total = total + chosen
            part = chosen[:8]
            for b in range(1, GROUP // 8):
                part = part + chosen[b * 8 : (b + 1) * 8]
            parts.append(part)
        kept_ref[:, q * QUAD : (q + 1) * QUAD] = total
    some = jnp.concatenate(parts, axis=0)
    high, rest = some.astype(BF16), some
    rest = rest - high.astype(F32)
    mid = rest.astype(BF16)
    low = (rest - mid.astype(F32)).astype(BF16)
    lanes = dot(jnp.concatenate([high, mid, low], axis=0), pack_ref[...])
    row = iota((128, 128), 0)
    lane = iota((128, 128), 1)
    fits = ((row % BLOCK) == (lane % BLOCK)) & (((row // 32) % 2) == (lane // 64))
    lanes = jnp.concatenate([jnp.where(fits, lanes[t * 128 : (t + 1) * 128], 0.0) for t in range(3)], axis=0)
    values = dot(fold_ref[...], lanes.astype(BF16))
    for d in range(send_ref.shape[0]):
        send_ref[d, pl.ds(pl.multiple_of(step * 8, 8), 8), :] = values

    @pl.when(step == 0)
    def _():
        padded = jnp.concatenate([picks8, jnp.full((8, 128 - groups), -1.0, F32)], axis=1)
        for d in range(send_ref.shape[0]):
            send_ref[d, ROWS - 8 : ROWS, :] = padded


def momentum_kernel(kept_ref, moment_ref, left_ref, right_ref, out_ref):
    back = times_right(stack_quads(times_left(left_ref[...], kept_ref[...])), right_ref)
    for q in range(back.shape[0] // GROUP):
        cols = slice(q * QUAD, (q + 1) * QUAD)
        out_ref[:, cols] = moment_ref[:, cols] - back[q * GROUP : (q + 1) * GROUP]


def update_kernel(core_ref, own_ref, other_ref, left_ref, right_ref, update_ref, energy_ref,
                  high_ref, low_ref, rows_ref, cols_ref, coef_ref, wide_ref):
    first = core_ref[0] == 0
    half = own_ref.shape[0] // ROWS

    def slab(r):
        a = own_ref[pl.ds(r, half, stride=ROWS), :]
        b = other_ref[pl.ds(r, half, stride=ROWS), :]
        return jnp.concatenate([jnp.where(first, a, b), jnp.where(first, b, a)], axis=0)

    def turned(r):
        return jnp.concatenate([
            jnp.concatenate([slab(r + k), slab(r + k + 1)], axis=0).T for k in range(0, KMAX, 2)
        ], axis=1)

    picks = turned(ROWS - 8)[:GROUP]
    row_block = jnp.floor(picks * (1.0 / SIDE))
    row_high = jnp.floor(row_block * 0.25)
    rows_ref[...] = row_block - 4.0 * row_high
    cols_ref[...] = row_high * SIDE + (picks - SIDE * row_block)
    for t in range(8):
        high, low = split(turned(t * KMAX))
        high_ref[t] = high
        low_ref[t] = low

    slot_of_lane = (iota((8, QUAD), 1) // SIDE) % BLOCK
    slot_of_row = iota((8, QUAD), 0) // BLOCK
    in_low = slot_of_lane == slot_of_row
    in_high = slot_of_lane == slot_of_row + 2
    upper = iota((8, QUAD), 0) < BLOCK
    block_of_row = iota((GROUP, QUAD), 0).astype(F32)

    def eight(t, energy):
        base = pl.multiple_of(t * 8, 8)
        rows8 = rows_ref[pl.ds(base, 8), :]
        cols8 = cols_ref[pl.ds(base, 8), :]
        for g in range(8):
            vals = [high_ref[t, g * 16 : (g + 1) * 16, :].astype(F32),
                    low_ref[t, g * 16 : (g + 1) * 16, :].astype(F32)]
            row = rows8[g : g + 1]
            left = jnp.concatenate([
                jnp.where(row == float(b), v, 0.0).astype(BF16) for b in range(4) for v in vals
            ], axis=0)
            onehot = jnp.where(block_of_row == cols8[g : g + 1], 1.0, 0.0).astype(BF16)
            right = jnp.concatenate([onehot[b * 16 : (b + 1) * 16] for b in range(4) for _ in range(BLOCK)], axis=0)
            out = lax.dot_general(left, right, (((1,), (1,)), ((), ())), preferred_element_type=F32)
            folded = []
            for b in range(4):
                both = out[b * 32 : b * 32 + 16] + out[b * 32 + 16 : b * 32 + 32]
                lanes = jnp.where(in_low, both[:8], jnp.where(in_high, both[8:], 0.0))
                folded.append(lanes + pltpu.roll(lanes, 4, 0))
            for b in range(0, 4, 2):
                coef = jnp.where(upper, folded[b], folded[b + 1])
                coef_ref[pl.ds(pl.multiple_of(t * 128 + g * 16 + b * 4, 8), 8), :] = coef
                energy = energy + coef * coef
        return energy

    energy = lax.fori_loop(0, 8, eight, jnp.zeros((8, QUAD), F32))
    energy_ref[...] = jnp.broadcast_to((energy[:, :128] + energy[:, 128:])[None], energy_ref.shape)
    half_lane = iota((16, 128), 1) < GROUP
    for t in range(4):
        back = times_right(coef_ref[t * QUAD : (t + 1) * QUAD, :], right_ref)
        for pair in range(8):
            even = back[pair * 32 : pair * 32 + 16]
            odd = back[pair * 32 + 16 : pair * 32 + 32]
            lanes = slice((t * 8 + pair) * 128, (t * 8 + pair + 1) * 128)
            for w in range(2):
                e = even[:, w * 128 : (w + 1) * 128]
                o = odd[:, w * 128 : (w + 1) * 128]
                wide_ref[w * 32 : w * 32 + 16, lanes] = jnp.where(half_lane, e, pltpu.roll(o, GROUP, 1))
                wide_ref[w * 32 + 16 : w * 32 + 32, lanes] = jnp.where(half_lane, pltpu.roll(e, GROUP, 1), o)
    for t in range(4):
        lanes = slice(t * 1024, (t + 1) * 1024)
        update_ref[:, lanes] = times_left(left_ref[...], wide_ref[:, lanes])


def weights_kernel(replicas, total_rows, energy_ref, update_ref, weights_ref, out_ref):
    energy = jnp.sum(energy_ref[0])
    for r in range(1, energy_ref.shape[0]):
        energy = energy + jnp.sum(energy_ref[r])
    mean = jnp.broadcast_to(energy * (1.0 / (replicas * replicas * total_rows)), (8, 128))
    factor = (0.5 / replicas) / jnp.sqrt(mean + 1e-06)
    out_ref[...] = weights_ref[...] - update_ref[...] * factor[:1, :1]


def whole(shape):
    return pl.BlockSpec(shape, lambda *_: (0,) * len(shape))


def on_device(momentum, grad, weights, picks, counts):
    width = weights.shape[1]
    nchunk = width // GROUP
    replicas = lax.axis_size("dp")
    nmp = lax.axis_size("mp")
    along_y, along_x, cores = 8, 4, 2
    mat = basis()
    step_width = 1024
    steps = width // step_width
    tile = pl.BlockSpec((GROUP, step_width), lambda s: (0, s))
    left_fwd = jnp.asarray(left_weights(mat))
    left_inv = jnp.asarray(left_weights(mat.T))
    right_fwd = jnp.asarray(right_weights(mat.T))
    right_inv = jnp.asarray(right_weights(mat))
    send, kept, moment = pl.pallas_call(
        send_kernel,
        grid=(steps,),
        in_specs=[tile, tile, whole((KMAX, nchunk)), whole((1, nchunk)), whole((GROUP, QUAD)),
                  whole((2, QUAD, QUAD)), whole((QUAD, 128)), whole((8, 384))],
        out_specs=[whole((along_y, ROWS, 128)), tile, tile],
        out_shape=[jax.ShapeDtypeStruct((along_y, ROWS, 128), F32),
                   jax.ShapeDtypeStruct((GROUP, width), F32),
                   jax.ShapeDtypeStruct((GROUP, width), F32)],
        compiler_params=PARAMS,
        name="send",
    )(momentum[0], grad[0], picks[0, 0].T, counts[0], left_fwd, right_fwd,
      jnp.asarray(pack_weights()), jnp.asarray(pack_rows()))

    def device(y, x, core):
        return (y * along_x + x) * cores + core

    rings_y = [[device(y, x, c) for y in range(along_y)] for x in range(along_x) for c in range(cores)]
    rings_x = [[device(y, x, c) for x in range(along_x)] for y in range(along_y) for c in range(cores)]
    got_y = lax.all_to_all(send, "dp", 0, 0, tiled=True, axis_index_groups=rings_y)
    again = jnp.broadcast_to(got_y.reshape(1, along_y * ROWS, 128), (along_x, along_y * ROWS, 128))
    got_x = lax.all_to_all(again, "dp", 0, 0, tiled=True, axis_index_groups=rings_x)
    own = got_x.reshape(along_x * along_y * ROWS, 128)

    new_momentum = pl.pallas_call(
        momentum_kernel,
        grid=(steps,),
        in_specs=[tile, tile, whole((GROUP, QUAD)), whole((2, QUAD, QUAD))],
        out_specs=tile,
        out_shape=jax.ShapeDtypeStruct((GROUP, width), F32),
        compiler_params=PARAMS,
        cost_estimate=pl.CostEstimate(flops=6 * 2 * 2 * GROUP * GROUP * width, bytes_accessed=12 * GROUP * width,
                                      transcendentals=0),
        name="momentum",
    )(kept, moment, left_inv, right_inv)

    other = lax.ppermute(own, "dp", [(p, p ^ 1) for p in range(replicas)])
    core = (lax.axis_index("dp") % cores).astype(jnp.int32).reshape(1)
    update, energy = pl.pallas_call(
        update_kernel,
        in_specs=[pl.BlockSpec(memory_space=pltpu.SMEM)] + [pl.BlockSpec(memory_space=pltpu.VMEM)] * 4,
        out_shape=[jax.ShapeDtypeStruct((GROUP, width), F32), jax.ShapeDtypeStruct((nmp, 8, 128), F32)],
        scratch_shapes=[
            pltpu.VMEM((8, 128, QUAD), BF16),
            pltpu.VMEM((8, 128, QUAD), BF16),
            pltpu.VMEM((nchunk, QUAD), F32),
            pltpu.VMEM((nchunk, QUAD), F32),
            pltpu.VMEM((nchunk * 16, QUAD), F32),
            pltpu.VMEM((GROUP, width), F32),
        ],
        compiler_params=PARAMS,
        name="update",
    )(core, own, other, left_inv, jnp.asarray(scatter_weights(mat)))
    energies = lax.all_to_all(energy, "mp", 0, 0, tiled=True)
    new_weights = pl.pallas_call(
        functools.partial(weights_kernel, float(replicas), float(GROUP * nmp * width)),
        out_shape=jax.ShapeDtypeStruct((GROUP, width), F32),
        compiler_params=PARAMS,
        name="weights",
    )(energies, update, weights)
    return (new_momentum[None], new_weights)


def solution(mesh):
    in_specs = (
        P("dp", "mp", None),
        P("dp", "mp", None),
        P("mp", None),
        P("dp", "mp", None, None),
        P("dp", "mp", None),
    )
    out_specs = (P("dp", "mp", None), P("mp", None))
    return jax.shard_map(
        on_device, mesh=mesh, in_specs=in_specs, out_specs=out_specs, check_vma=False
    )
```

```python
import functools

import jax
import jax.numpy as jnp
import ml_dtypes
import numpy as np
from jax import lax
from jax.experimental import pallas as pl
from jax.experimental.pallas import tpu as pltpu
from jax.sharding import PartitionSpec as P

GROUP = 64
BLOCK = 4
KMAX = 4
SIDE = GROUP // BLOCK
QUAD = 4 * GROUP
ROWS = 17
F32 = jnp.float32
BF16 = jnp.bfloat16
PARAMS = pltpu.CompilerParams(vmem_limit_bytes=24 * 1024 * 1024)


def basis():
    rows = np.arange(GROUP, dtype=np.float64)[:, None]
    cols = np.arange(GROUP, dtype=np.float64)[None, :]
    waves = np.cos(np.pi * (2.0 * cols + 1.0) * rows / (2.0 * GROUP))
    factor = np.where(rows == 0.0, np.sqrt(1.0 / GROUP), np.sqrt(2.0 / GROUP))
    return (waves * factor).astype(np.float32)


def halves(mat):
    high = mat.astype(ml_dtypes.bfloat16)
    low = (mat - high.astype(np.float32)).astype(ml_dtypes.bfloat16)
    return high, low


def left_weights(mat):
    high, low = halves(mat)
    return np.concatenate([high, high, low, low], axis=1)


def right_weights(mat):
    return np.stack(halves(np.kron(np.eye(4, dtype=np.float32), mat)))


def scatter_weights(mat):
    perm = np.arange(GROUP).reshape(SIDE, BLOCK).T.reshape(-1)
    return right_weights(mat[perm])


def iota(shape, axis):
    return lax.broadcasted_iota(jnp.int32, shape, axis)


def dot(a, b):
    return jnp.dot(a, b, preferred_element_type=F32)


def split(x):
    high = x.astype(BF16)
    return high, (x - high.astype(F32)).astype(BF16)


def times_left(weights, x):
    high, low = split(x)
    return dot(weights, jnp.concatenate([high, low, high, low], axis=0))


def stack_quads(x):
    return jnp.concatenate([x[:, q * QUAD : (q + 1) * QUAD] for q in range(x.shape[1] // QUAD)], axis=0)


def transform_weights(left, right):
    return np.concatenate([left, right[0], right[1]], axis=0)


def times_right(x, weights):
    high, low = split(x)
    top = weights[GROUP : GROUP + QUAD]
    return dot(high, top) + (dot(low, top) + dot(high, weights[GROUP + QUAD :]))


def flag(cond):
    return jnp.where(cond, 1.0, 0.0).astype(BF16)


def numbers():
    number = (iota((GROUP, QUAD), 0) // BLOCK) * SIDE + (iota((GROUP, QUAD), 1) % GROUP) // BLOCK
    return number.astype(F32)


def listed(picks, counts):
    valid = iota(picks.shape, 0) < counts
    return jnp.where(valid, picks.astype(F32), -1.0)


def spread_lanes(picks, width, start):
    groups = picks.shape[1]
    eight = jnp.concatenate([picks, jnp.full_like(picks, -1.0)], axis=0).astype(BF16)
    member = flag(iota((groups, width), 0) == start + iota((groups, width), 1) // GROUP)
    return dot(eight, member)


def send_kernel(mom_hbm, grad_hbm, picks_hbm, counts_hbm, weights_hbm, send_ref,
                mom_ref, grad_ref, picks_ref, counts_ref, weights_ref, sems):
    copies = [
        pltpu.make_async_copy(src, dst, sems.at[i])
        for i, (src, dst) in enumerate((
            (picks_hbm, picks_ref), (counts_hbm, counts_ref), (weights_hbm, weights_ref),
            (mom_hbm, mom_ref), (grad_hbm, grad_ref)))
    ]
    for copy in copies:
        copy.start()
    width = mom_ref.shape[1]
    quads = width // QUAD

    row = iota((QUAD, 128), 0)
    lane = iota((QUAD, 128), 1)
    pack = flag((row // GROUP == (lane // 16) % 4) & (row % BLOCK == (lane // BLOCK) % BLOCK))
    row = iota((8, 384), 0)
    lane = iota((8, 384), 1)
    fold = flag((row // KMAX == (lane % 128) // 64) & (row % KMAX == (lane // 8) % KMAX))
    row = iota((128, 128), 0)
    lane = iota((128, 128), 1)
    fits = ((row % BLOCK) == (lane % BLOCK)) & (((row // 32) % 2) == (lane // 64))
    number = numbers()

    for copy in copies[:3]:
        copy.wait()
    picks = listed(picks_ref[...], counts_ref[...])
    groups = picks.shape[1]
    wide = spread_lanes(picks, width, 0)
    weights = weights_ref[...]
    for copy in copies[3:]:
        copy.wait()
    moment = 0.9 * mom_ref[...] + grad_ref[...].astype(F32)
    coef = times_right(stack_quads(times_left(weights[:GROUP], moment)), weights)
    packed = []
    for first in range(0, quads, 4):
        parts = []
        for q in range(first, first + 4):
            quad = coef[q * GROUP : (q + 1) * GROUP]
            for k in range(KMAX):
                chosen = jnp.where(number == wide[k : k + 1, q * QUAD : (q + 1) * QUAD], quad, 0.0)
                some = chosen[:8]
                for b in range(1, GROUP // 8):
                    some = some + chosen[b * 8 : (b + 1) * 8]
                parts.append(some)
        some = jnp.concatenate(parts, axis=0)
        high = some.astype(BF16)
        rest = some - high.astype(F32)
        mid = rest.astype(BF16)
        low = (rest - mid.astype(F32)).astype(BF16)
        lanes = dot(jnp.concatenate([high, mid, low], axis=0), pack)
        lanes = jnp.concatenate([jnp.where(fits, lanes[t * 128 : (t + 1) * 128], 0.0) for t in range(3)], axis=0)
        packed.append(dot(fold, lanes.astype(BF16)))
    part = groups // 2
    both = []
    for h in range(2):
        row = jnp.concatenate([picks[k : k + 1, h * part : (h + 1) * part] for k in range(KMAX)], axis=1)
        both += [packed[2 * h], packed[2 * h + 1], row]
    again = jnp.concatenate(both * 4, axis=0)
    for d in range(send_ref.shape[0] // again.shape[0]):
        send_ref[d * again.shape[0] : (d + 1) * again.shape[0], :] = again


def momentum_kernel(mom_ref, grad_ref, picks_ref, counts_ref, forward_ref, inverse_ref, out_ref):
    width = mom_ref.shape[1]
    picks = listed(picks_ref[...], counts_ref[...])
    wide = spread_lanes(picks, width, pl.program_id(0) * (width // GROUP))
    forward = forward_ref[...]
    inverse = inverse_ref[...]
    number = numbers()
    moment = 0.9 * mom_ref[...] + grad_ref[...].astype(F32)
    coef = times_right(stack_quads(times_left(forward[:GROUP], moment)), forward)
    kept = []
    for q in range(width // QUAD):
        lanes = wide[:, q * QUAD : (q + 1) * QUAD]
        hit = number == lanes[:1]
        for k in range(1, KMAX):
            hit = hit | (number == lanes[k : k + 1])
        kept.append(jnp.where(hit, coef[q * GROUP : (q + 1) * GROUP], 0.0))
    back = times_right(stack_quads(times_left(inverse[:GROUP], jnp.concatenate(kept, axis=1))), inverse)
    for q in range(width // QUAD):
        cols = slice(q * QUAD, (q + 1) * QUAD)
        out_ref[:, cols] = moment[:, cols] - back[q * GROUP : (q + 1) * GROUP]


def scatter_kernel(got_ref, _, coef_ref, energy_ref, high_ref, low_ref, rows_ref, cols_ref):
    replicas = got_ref.shape[0] // ROWS
    eights = (ROWS - 1) // KMAX
    groups = eights * 8

    def slab(r):
        return got_ref[pl.ds(r, replicas, stride=ROWS), :]

    picks = slab(ROWS - 1)
    picks = jnp.concatenate([picks, picks], axis=0).T
    first = iota((groups, 128), 1) < replicas
    picks = jnp.concatenate([
        jnp.where(first, picks[k * groups : (k + 1) * groups], picks[(k + 1) * groups : (k + 2) * groups])
        for k in range(0, KMAX, 2)
    ], axis=1)
    row_block = jnp.floor(picks * (1.0 / SIDE))
    row_high = jnp.floor(row_block * 0.25)
    rows_ref[...] = row_block - 4.0 * row_high
    cols_ref[...] = row_high * SIDE + (picks - SIDE * row_block)
    for t in range(eights):
        turned = jnp.concatenate([
            jnp.concatenate([slab(t * KMAX + k), slab(t * KMAX + k + 1)], axis=0).T for k in range(0, KMAX, 2)
        ], axis=1)
        high, low = split(turned)
        high_ref[t] = high
        low_ref[t] = low

    slot_of_lane = (iota((8, QUAD), 1) // SIDE) % BLOCK
    slot_of_row = iota((8, QUAD), 0) // BLOCK
    in_low = slot_of_lane == slot_of_row
    in_high = slot_of_lane == slot_of_row + 2
    upper = iota((8, QUAD), 0) < BLOCK
    block_of_row = iota((GROUP, QUAD), 0).astype(F32)

    def eight(t, energy):
        base = pl.multiple_of(t * 8, 8)
        rows8 = rows_ref[pl.ds(base, 8), :]
        cols8 = cols_ref[pl.ds(base, 8), :]
        for g in range(8):
            vals = [high_ref[t, g * 16 : (g + 1) * 16, :].astype(F32),
                    low_ref[t, g * 16 : (g + 1) * 16, :].astype(F32)]
            row = rows8[g : g + 1]
            left = jnp.concatenate([
                jnp.where(row == float(b), v, 0.0).astype(BF16) for b in range(4) for v in vals
            ], axis=0)
            onehot = flag(block_of_row == cols8[g : g + 1])
            right = jnp.concatenate([onehot[b * 16 : (b + 1) * 16] for b in range(4) for _ in range(BLOCK)], axis=0)
            out = lax.dot_general(left, right, (((1,), (1,)), ((), ())), preferred_element_type=F32)
            folded = []
            for b in range(4):
                both = out[b * 32 : b * 32 + 16] + out[b * 32 + 16 : b * 32 + 32]
                lanes = jnp.where(in_low, both[:8], jnp.where(in_high, both[8:], 0.0))
                folded.append(lanes + pltpu.roll(lanes, 4, 0))
            for b in range(0, 4, 2):
                coef = jnp.where(upper, folded[b], folded[b + 1])
                coef_ref[pl.ds(pl.multiple_of(t * 128 + g * 16 + b * 4, 8), 8), :] = coef
                energy = energy + coef * coef
        return energy

    energy = lax.fori_loop(0, eights, eight, jnp.zeros((8, QUAD), F32))
    energy = jnp.sum(energy[:, :128] + energy[:, 128:], axis=0, keepdims=True)
    energy_ref[...] = jnp.broadcast_to(energy, energy_ref.shape)


def inverse_kernel(coef_ref, weights_ref, update_ref, wide_ref):
    weights = weights_ref[...]
    half_lane = iota((16, 128), 1) < GROUP
    for t in range(coef_ref.shape[0] // QUAD):
        back = times_right(coef_ref[t * QUAD : (t + 1) * QUAD, :], weights)
        for pair in range(8):
            even = back[pair * 32 : pair * 32 + 16]
            odd = back[pair * 32 + 16 : pair * 32 + 32]
            lanes = slice((t * 8 + pair) * 128, (t * 8 + pair + 1) * 128)
            for w in range(2):
                e = even[:, w * 128 : (w + 1) * 128]
                o = odd[:, w * 128 : (w + 1) * 128]
                wide_ref[w * 32 : w * 32 + 16, lanes] = jnp.where(half_lane, e, pltpu.roll(o, GROUP, 1))
                wide_ref[w * 32 + 16 : w * 32 + 32, lanes] = jnp.where(half_lane, pltpu.roll(e, GROUP, 1), o)
        lanes = slice(t * 1024, (t + 1) * 1024)
        update_ref[:, lanes] = times_left(weights[:GROUP], wide_ref[:, lanes])


def weights_kernel(replicas, total_rows, core_ref, energy_ref, own_ref, other_ref, weights_ref, out_ref):
    mean = jnp.broadcast_to(jnp.sum(energy_ref[...]) * (1.0 / (replicas * replicas * total_rows)), (8, 128))
    factor = ((0.5 / replicas) / jnp.sqrt(mean + 1e-06))[:1, :1]
    half = own_ref.shape[1]
    mine = core_ref[0] * half
    for mult, ref in ((mine, own_ref), (half - mine, other_ref)):
        cols = pl.ds(pl.multiple_of(mult, half), half)
        out_ref[:, cols] = weights_ref[:, cols] - ref[...] * factor


def whole(shape):
    return pl.BlockSpec(shape, lambda *_: (0,) * len(shape))


def on_device(momentum, grad, weights, picks, counts):
    width = weights.shape[1]
    nchunk = width // GROUP
    replicas = lax.axis_size("dp")
    nmp = lax.axis_size("mp")
    mat = basis()
    step_width = 1024
    steps = width // step_width
    half = width // 2
    tile = pl.BlockSpec((GROUP, step_width), lambda s: (0, s))
    forward = jnp.asarray(transform_weights(left_weights(mat), right_weights(mat.T)))
    inverse = jnp.asarray(transform_weights(left_weights(mat.T), right_weights(mat)))
    scatter = jnp.asarray(transform_weights(left_weights(mat.T), scatter_weights(mat)))
    hbm = pl.BlockSpec(memory_space=pltpu.HBM)
    vmem = pl.BlockSpec(memory_space=pltpu.VMEM)
    taken = [pltpu.with_memory_space_constraint(x, pltpu.HBM)
             for x in (momentum[0], grad[0], picks[0, 0].T, counts[0], forward)]
    send = pl.pallas_call(
        send_kernel,
        in_specs=[hbm] * 5,
        out_shape=jax.ShapeDtypeStruct((replicas * ROWS, 128), F32),
        scratch_shapes=[
            pltpu.VMEM((GROUP, width), F32),
            pltpu.VMEM((GROUP, width), BF16),
            pltpu.VMEM((KMAX, nchunk), jnp.int32),
            pltpu.VMEM((1, nchunk), jnp.int32),
            pltpu.VMEM(forward.shape, BF16),
            pltpu.SemaphoreType.DMA((5,)),
        ],
        compiler_params=PARAMS,
        name="send",
    )(*taken)

    got = lax.all_to_all(send.reshape(replicas * ROWS, 1, 128), "dp", 0, 0, tiled=True)
    new_momentum = pl.pallas_call(
        momentum_kernel,
        grid=(steps,),
        in_specs=[tile, tile, whole((KMAX, nchunk)), whole((1, nchunk)), whole(forward.shape), whole(inverse.shape)],
        out_specs=tile,
        out_shape=jax.ShapeDtypeStruct((GROUP, width), F32),
        compiler_params=PARAMS,
        cost_estimate=pl.CostEstimate(flops=12 * 2 * 2 * GROUP * GROUP * width, bytes_accessed=10 * GROUP * width,
                                      transcendentals=0),
        name="momentum",
    )(*taken, pltpu.with_memory_space_constraint(inverse, pltpu.HBM))
    coef, energy = pl.pallas_call(
        scatter_kernel,
        in_specs=[vmem, hbm],
        out_shape=[jax.ShapeDtypeStruct((half // 4, QUAD), F32), jax.ShapeDtypeStruct((2 * nmp, 128), F32)],
        scratch_shapes=[
            pltpu.VMEM((nchunk // 16, 128, QUAD), BF16),
            pltpu.VMEM((nchunk // 16, 128, QUAD), BF16),
            pltpu.VMEM((nchunk // 2, QUAD), F32),
            pltpu.VMEM((nchunk // 2, QUAD), F32),
        ],
        compiler_params=PARAMS,
        name="scatter",
    )(got.reshape(replicas * ROWS, 128), pltpu.with_memory_space_constraint(new_momentum, pltpu.HBM))
    partners = [[(2 * chip + core) * nmp + z for core in range(2) for z in range(nmp)] for chip in range(replicas // 2)]
    energies = lax.all_to_all(energy.reshape(2 * nmp, 1, 128), ("dp", "mp"), 0, 0, tiled=True,
                              axis_index_groups=partners).reshape(2 * nmp, 128)
    own = pl.pallas_call(
        inverse_kernel,
        out_shape=jax.ShapeDtypeStruct((GROUP, half), F32),
        scratch_shapes=[pltpu.VMEM((GROUP, half), F32)],
        compiler_params=PARAMS,
        cost_estimate=pl.CostEstimate(flops=6 * 2 * GROUP * GROUP * half, bytes_accessed=8 * GROUP * half,
                                      transcendentals=0),
        name="inverse",
    )(coef, scatter)
    other = lax.ppermute(own, "dp", [(p, p ^ 1) for p in range(replicas)])
    core = jnp.bitwise_and(lax.axis_index("dp"), 1).astype(jnp.int32).reshape(1)
    new_weights = pl.pallas_call(
        functools.partial(weights_kernel, float(replicas), float(GROUP * nmp * width)),
        in_specs=[pl.BlockSpec(memory_space=pltpu.SMEM)] + [vmem] * 4,
        out_shape=jax.ShapeDtypeStruct((GROUP, width), F32),
        compiler_params=PARAMS,
        name="weights",
    )(core, energies, own, other, weights)
    return (new_momentum[None], new_weights)


def solution(mesh):
    in_specs = (
        P("dp", "mp", None),
        P("dp", "mp", None),
        P("mp", None),
        P("dp", "mp", None, None),
        P("dp", "mp", None),
    )
    out_specs = (P("dp", "mp", None), P("mp", None))
    return jax.shard_map(
        on_device, mesh=mesh, in_specs=in_specs, out_specs=out_specs, check_vma=False
    )
```

```python
import functools

import jax
import jax.numpy as jnp
import ml_dtypes
import numpy as np
from jax import lax
from jax.experimental import pallas as pl
from jax.experimental.pallas import tpu as pltpu
from jax.sharding import PartitionSpec as P

GROUP = 64
BLOCK = 4
KMAX = 4
SIDE = GROUP // BLOCK
QUAD = 4 * GROUP
ROWS = 17
F32 = jnp.float32
BF16 = jnp.bfloat16
PARAMS = pltpu.CompilerParams(vmem_limit_bytes=24 * 1024 * 1024)


def basis():
    rows = np.arange(GROUP, dtype=np.float64)[:, None]
    cols = np.arange(GROUP, dtype=np.float64)[None, :]
    waves = np.cos(np.pi * (2.0 * cols + 1.0) * rows / (2.0 * GROUP))
    factor = np.where(rows == 0.0, np.sqrt(1.0 / GROUP), np.sqrt(2.0 / GROUP))
    return (waves * factor).astype(np.float32)


def halves(mat):
    high = mat.astype(ml_dtypes.bfloat16)
    low = (mat - high.astype(np.float32)).astype(ml_dtypes.bfloat16)
    return high, low


def left_weights(mat):
    high, low = halves(mat)
    return np.concatenate([high, high, low, low], axis=1)


def right_weights(mat):
    return np.stack(halves(np.kron(np.eye(4, dtype=np.float32), mat)))


def scatter_weights(mat):
    four = np.kron(np.eye(4, dtype=np.float32), mat)
    order = np.arange(QUAD).reshape(4, SIDE, BLOCK).transpose(2, 0, 1).reshape(-1)
    return np.stack(halves(four[order]))


def iota(shape, axis):
    return lax.broadcasted_iota(jnp.int32, shape, axis)


def dot(a, b):
    return jnp.dot(a, b, preferred_element_type=F32)


def split(x):
    high = x.astype(BF16)
    return high, (x - high.astype(F32)).astype(BF16)


def times_left(weights, x):
    high, low = split(x)
    return dot(weights, jnp.concatenate([high, low, high, low], axis=0))


def stack_quads(x):
    return jnp.concatenate([x[:, q * QUAD : (q + 1) * QUAD] for q in range(x.shape[1] // QUAD)], axis=0)


def transform_weights(left, right):
    return np.concatenate([left, right[0], right[1]], axis=0)


def times_right(x, weights):
    high, low = split(x)
    top = weights[GROUP : GROUP + QUAD]
    return dot(high, top) + (dot(low, top) + dot(high, weights[GROUP + QUAD :]))


def flag(cond):
    return jnp.where(cond, 1.0, 0.0).astype(BF16)


def numbers():
    number = (iota((GROUP, QUAD), 0) // BLOCK) * SIDE + (iota((GROUP, QUAD), 1) % GROUP) // BLOCK
    return number.astype(F32)


def listed(picks, counts):
    valid = iota(picks.shape, 0) < counts
    return jnp.where(valid, picks.astype(F32), -1.0)


def spread_lanes(picks, width, start):
    groups = picks.shape[1]
    eight = jnp.concatenate([picks, jnp.full_like(picks, -1.0)], axis=0).astype(BF16)
    member = flag(iota((groups, width), 0) == start + iota((groups, width), 1) // GROUP)
    return dot(eight, member)


def send_kernel(mom_hbm, grad_hbm, picks_hbm, counts_hbm, weights_hbm, send_ref,
                mom_ref, grad_ref, picks_ref, counts_ref, weights_ref, sems):
    width = mom_ref.shape[1]
    pairs = ((picks_hbm, picks_ref), (counts_hbm, counts_ref), (weights_hbm, weights_ref),
             (mom_hbm, mom_ref), (grad_hbm, grad_ref))
    copies = [pltpu.make_async_copy(src, dst, sems.at[i]) for i, (src, dst) in enumerate(pairs)]
    for copy in copies:
        copy.start()

    row = iota((QUAD, 128), 0)
    lane = iota((QUAD, 128), 1)
    pack = flag((row // GROUP == (lane // 16) % 4) & (row % BLOCK == (lane // BLOCK) % BLOCK))
    row = iota((8, 256), 0)
    lane = iota((8, 256), 1)
    fold = flag((row // KMAX == (lane % 128) // 64) & (row % KMAX == (lane // 8) % KMAX))
    row = iota((128, 128), 0)
    lane = iota((128, 128), 1)
    fits = ((row % BLOCK) == (lane % BLOCK)) & (((row // 32) % 2) == (lane // 64))
    number = numbers()

    for copy in copies[:3]:
        copy.wait()
    picks = listed(picks_ref[...], counts_ref[...])
    groups = picks.shape[1]
    wide = spread_lanes(picks, width, 0)
    weights = weights_ref[...]

    for copy in copies[3:]:
        copy.wait()

    moment = 0.9 * mom_ref[...] + grad_ref[...].astype(F32)
    coef = times_right(stack_quads(times_left(weights[:GROUP], moment)), weights)
    done = []
    for first in range(0, width // QUAD, 4):
        parts = []
        for q in range(first, first + 4):
            quad = coef[q * GROUP : (q + 1) * GROUP]
            for k in range(KMAX):
                pick = wide[k : k + 1, q * QUAD : (q + 1) * QUAD]
                some = jnp.zeros((8, QUAD), F32)
                for b in range(GROUP // 8):
                    rows = slice(b * 8, (b + 1) * 8)
                    some = jnp.where(number[rows] == pick, quad[rows], some)
                parts.append(some)
        lanes = dot(jnp.concatenate(split(jnp.concatenate(parts, axis=0)), axis=0), pack)
        lanes = jnp.concatenate([jnp.where(fits, lanes[t * 128 : (t + 1) * 128], 0.0) for t in range(2)], axis=0)
        done.append(dot(fold, lanes.astype(BF16)))
    part = groups // 2
    both = []
    for h in range(2):
        row = jnp.concatenate([picks[k : k + 1, h * part : (h + 1) * part] for k in range(KMAX)], axis=1)
        both += [done[2 * h], done[2 * h + 1], row]
    again = jnp.concatenate(both * 4, axis=0)
    for d in range(send_ref.shape[0] // again.shape[0]):
        send_ref[d * again.shape[0] : (d + 1) * again.shape[0], :] = again


def momentum_kernel(mom_ref, grad_ref, picks_ref, counts_ref, forward_ref, inverse_ref, out_ref):
    width = mom_ref.shape[1]
    picks = listed(picks_ref[...], counts_ref[...])
    wide = spread_lanes(picks, width, pl.program_id(0) * (width // GROUP))
    forward = forward_ref[...]
    inverse = inverse_ref[...]
    number = numbers()
    moment = 0.9 * mom_ref[...] + grad_ref[...].astype(F32)
    coef = times_right(stack_quads(times_left(forward[:GROUP], moment)), forward)
    kept = []
    for q in range(width // QUAD):
        lanes = wide[:, q * QUAD : (q + 1) * QUAD]
        hit = number == lanes[:1]
        for k in range(1, KMAX):
            hit = hit | (number == lanes[k : k + 1])
        kept.append(jnp.where(hit, coef[q * GROUP : (q + 1) * GROUP], 0.0))
    back = times_right(stack_quads(times_left(inverse[:GROUP], jnp.concatenate(kept, axis=1))), inverse)
    for q in range(width // QUAD):
        cols = slice(q * QUAD, (q + 1) * QUAD)
        out_ref[:, cols] = moment[:, cols] - back[q * GROUP : (q + 1) * GROUP]


def scatter_kernel(got_ref, _, coef_ref, energy_ref, high_ref, low_ref, rows_ref, cols_ref):
    replicas = got_ref.shape[0] // ROWS
    eights = (ROWS - 1) // KMAX
    groups = eights * 8

    def slab(r):
        return got_ref[pl.ds(r, replicas, stride=ROWS), :]

    picks = slab(ROWS - 1)
    picks = jnp.concatenate([picks, picks], axis=0).T
    first = iota((groups, 128), 1) < replicas
    picks = jnp.concatenate([
        jnp.where(first, picks[k * groups : (k + 1) * groups], picks[(k + 1) * groups : (k + 2) * groups])
        for k in range(0, KMAX, 2)
    ], axis=1)
    row_block = jnp.floor(picks * (1.0 / SIDE))
    row_high = jnp.floor(row_block * 0.25)
    rows_ref[...] = row_block - 4.0 * row_high
    cols_ref[...] = row_high * SIDE + (picks - SIDE * row_block)
    for t in range(eights):
        turned = jnp.concatenate([
            jnp.concatenate([slab(t * KMAX + k), slab(t * KMAX + k + 1)], axis=0).T for k in range(0, KMAX, 2)
        ], axis=1)
        high, low = split(turned)
        high_ref[t] = high
        low_ref[t] = low

    upper = iota((8, 128), 0) < BLOCK
    early = iota((8, 128), 1) < GROUP
    block_of_row = iota((GROUP, QUAD), 0).astype(F32)

    def eight(t, energy):
        base = pl.multiple_of(t * 8, 8)
        rows8 = rows_ref[pl.ds(base, 8), :]
        cols8 = cols_ref[pl.ds(base, 8), :]
        for g in range(8):
            vals = [high_ref[t, g * 16 : (g + 1) * 16, :], low_ref[t, g * 16 : (g + 1) * 16, :]]
            row = jnp.broadcast_to(rows8[g : g + 1], (16, QUAD))
            masks = [flag(row == float(b)) for b in range(4)]
            left = jnp.concatenate([m * v for m in masks for v in vals], axis=0)
            onehot = flag(block_of_row == cols8[g : g + 1])
            right = jnp.concatenate([onehot, onehot], axis=0)
            out = lax.dot_general(left, right, (((1,), (1,)), ((), ())), preferred_element_type=F32)
            both = [out[b * 32 : b * 32 + 16] + out[b * 32 + 16 : b * 32 + 32] for b in range(4)]
            for b in range(0, 4, 2):
                for j in range(2):
                    one, two = both[b][j * 8 : j * 8 + 8], both[b + 1][j * 8 : j * 8 + 8]
                    first = jnp.where(upper, one, pltpu.roll(two, BLOCK, 0))
                    second = jnp.where(upper, pltpu.roll(one, BLOCK, 0), two)
                    coef = jnp.where(early, first, second)
                    coef_ref[pl.ds(pl.multiple_of(t * 128 + g * 16 + b * 4, 8), 8), j * 128 : (j + 1) * 128] = coef
                    energy = energy + coef * coef
        return energy

    energy = lax.fori_loop(0, eights, eight, jnp.zeros((8, 128), F32), unroll=True)
    energy = jnp.sum(energy, axis=0, keepdims=True)
    energy_ref[...] = jnp.broadcast_to(energy, energy_ref.shape)


def inverse_kernel(core_ref, own_ref, other_ref, weights_ref, update_ref, wide_ref):
    weights = weights_ref[...]
    half_lane = iota((16, 128), 1) < GROUP
    half = update_ref.shape[1] // 2
    mine = core_ref[0] * half
    for coef_ref, start in ((own_ref, mine), (other_ref, half - mine)):
        for t in range(coef_ref.shape[0] // QUAD):
            back = times_right(coef_ref[t * QUAD : (t + 1) * QUAD, :], weights)
            for pair in range(8):
                even = back[pair * 32 : pair * 32 + 16]
                odd = back[pair * 32 + 16 : pair * 32 + 32]
                lanes = slice(pair * 128, (pair + 1) * 128)
                for w in range(2):
                    e = even[:, w * 128 : (w + 1) * 128]
                    o = odd[:, w * 128 : (w + 1) * 128]
                    wide_ref[w * 32 : w * 32 + 16, lanes] = jnp.where(half_lane, e, pltpu.roll(o, GROUP, 1))
                    wide_ref[w * 32 + 16 : w * 32 + 32, lanes] = jnp.where(half_lane, pltpu.roll(e, GROUP, 1), o)
            update_ref[:, pl.ds(pl.multiple_of(start + t * 1024, 1024), 1024)] = times_left(
                weights[:GROUP], wide_ref[...])


def weights_kernel(replicas, total_rows, energy_ref, update_ref, weights_ref, out_ref):
    mean = jnp.broadcast_to(jnp.sum(energy_ref[...]) * (1.0 / (replicas * replicas * total_rows)), (8, 128))
    factor = ((0.5 / replicas) / jnp.sqrt(mean + 1e-06))[:1, :1]
    out_ref[...] = weights_ref[...] - update_ref[...] * factor


def whole(shape):
    return pl.BlockSpec(shape, lambda *_: (0,) * len(shape))


def on_device(momentum, grad, weights, picks, counts):
    width = weights.shape[1]
    nchunk = width // GROUP
    replicas = lax.axis_size("dp")
    nmp = lax.axis_size("mp")
    mat = basis()
    step_width = 1024
    steps = width // step_width
    half = width // 2
    tile = pl.BlockSpec((GROUP, step_width), lambda s: (0, s))
    forward = jnp.asarray(transform_weights(left_weights(mat), right_weights(mat.T)))
    inverse = jnp.asarray(transform_weights(left_weights(mat.T), right_weights(mat)))
    scatter = jnp.asarray(transform_weights(left_weights(mat.T), scatter_weights(mat)))
    hbm = pl.BlockSpec(memory_space=pltpu.HBM)
    vmem = pl.BlockSpec(memory_space=pltpu.VMEM)
    taken = [pltpu.with_memory_space_constraint(x, pltpu.HBM)
             for x in (momentum[0], grad[0], picks[0, 0].T, counts[0], forward)]
    send = pl.pallas_call(
        send_kernel,
        in_specs=[hbm] * 5,
        out_shape=jax.ShapeDtypeStruct((replicas * ROWS, 128), F32),
        scratch_shapes=[
            pltpu.VMEM((GROUP, width), F32),
            pltpu.VMEM((GROUP, width), BF16),
            pltpu.VMEM((KMAX, nchunk), jnp.int32),
            pltpu.VMEM((1, nchunk), jnp.int32),
            pltpu.VMEM(forward.shape, BF16),
            pltpu.SemaphoreType.DMA((5,)),
        ],
        compiler_params=PARAMS,
        name="send",
    )(*taken)

    got = lax.all_to_all(send.reshape(replicas * ROWS, 1, 128), "dp", 0, 0, tiled=True)
    new_momentum = pl.pallas_call(
        momentum_kernel,
        grid=(steps,),
        in_specs=[tile, tile, whole((KMAX, nchunk)), whole((1, nchunk)), whole(forward.shape), whole(inverse.shape)],
        out_specs=tile,
        out_shape=jax.ShapeDtypeStruct((GROUP, width), F32),
        compiler_params=PARAMS,
        cost_estimate=pl.CostEstimate(flops=12 * 2 * 2 * GROUP * GROUP * width, bytes_accessed=10 * GROUP * width,
                                      transcendentals=0),
        name="momentum",
    )(*taken, pltpu.with_memory_space_constraint(inverse, pltpu.HBM))
    coef, energy = pl.pallas_call(
        scatter_kernel,
        in_specs=[vmem, hbm],
        out_shape=[jax.ShapeDtypeStruct((half // 4, QUAD), F32), jax.ShapeDtypeStruct((2 * nmp, 128), F32)],
        scratch_shapes=[
            pltpu.VMEM((nchunk // 16, 128, QUAD), BF16),
            pltpu.VMEM((nchunk // 16, 128, QUAD), BF16),
            pltpu.VMEM((nchunk // 2, QUAD), F32),
            pltpu.VMEM((nchunk // 2, QUAD), F32),
        ],
        compiler_params=PARAMS,
        name="scatter",
    )(got.reshape(replicas * ROWS, 128), pltpu.with_memory_space_constraint(new_momentum, pltpu.HBM))
    partners = [[(2 * chip + core) * nmp + z for core in range(2) for z in range(nmp)] for chip in range(replicas // 2)]
    energies = lax.all_to_all(energy.reshape(2 * nmp, 1, 128), ("dp", "mp"), 0, 0, tiled=True,
                              axis_index_groups=partners).reshape(2 * nmp, 128)
    other = lax.ppermute(coef, "dp", [(p, p ^ 1) for p in range(replicas)])
    core = jnp.bitwise_and(lax.axis_index("dp"), 1).astype(jnp.int32).reshape(1)
    update = pl.pallas_call(
        inverse_kernel,
        in_specs=[pl.BlockSpec(memory_space=pltpu.SMEM)] + [vmem] * 3,
        out_shape=jax.ShapeDtypeStruct((GROUP, width), F32),
        scratch_shapes=[pltpu.VMEM((GROUP, 1024), F32)],
        compiler_params=PARAMS,
        cost_estimate=pl.CostEstimate(flops=6 * 2 * 2 * GROUP * GROUP * width, bytes_accessed=8 * GROUP * width,
                                      transcendentals=0),
        name="inverse",
    )(core, coef, other, scatter)
    new_weights = pl.pallas_call(
        functools.partial(weights_kernel, float(replicas), float(GROUP * nmp * width)),
        out_shape=jax.ShapeDtypeStruct((GROUP, width), F32),
        compiler_params=PARAMS,
        name="weights",
    )(energies, update, weights)
    return (new_momentum[None], new_weights)


def solution(mesh):
    in_specs = (
        P("dp", "mp", None),
        P("dp", "mp", None),
        P("mp", None),
        P("dp", "mp", None, None),
        P("dp", "mp", None),
    )
    out_specs = (P("dp", "mp", None), P("mp", None))
    return jax.shard_map(
        on_device, mesh=mesh, in_specs=in_specs, out_specs=out_specs, check_vma=False
    )
```

```python
import functools

import jax
import jax.numpy as jnp
import ml_dtypes
import numpy as np
from jax import lax
from jax.experimental import pallas as pl
from jax.experimental.pallas import tpu as pltpu
from jax.sharding import PartitionSpec as P

GROUP = 64
BLOCK = 4
KMAX = 4
SIDE = GROUP // BLOCK
QUAD = 4 * GROUP
ROWS = 17
F32 = jnp.float32
BF16 = jnp.bfloat16
PARAMS = pltpu.CompilerParams(vmem_limit_bytes=24 * 1024 * 1024)


def basis():
    rows = np.arange(GROUP, dtype=np.float64)[:, None]
    cols = np.arange(GROUP, dtype=np.float64)[None, :]
    waves = np.cos(np.pi * (2.0 * cols + 1.0) * rows / (2.0 * GROUP))
    factor = np.where(rows == 0.0, np.sqrt(1.0 / GROUP), np.sqrt(2.0 / GROUP))
    return (waves * factor).astype(np.float32)


def halves(mat):
    high = mat.astype(ml_dtypes.bfloat16)
    low = (mat - high.astype(np.float32)).astype(ml_dtypes.bfloat16)
    return high, low


def left_weights(mat):
    high, low = halves(mat)
    return np.concatenate([high, high, low, low], axis=1)


def right_weights(mat):
    return np.stack(halves(np.kron(np.eye(4, dtype=np.float32), mat)))


def scatter_weights(mat):
    four = np.kron(np.eye(4, dtype=np.float32), mat)
    order = np.arange(QUAD).reshape(4, SIDE, BLOCK).transpose(2, 0, 1).reshape(-1)
    return np.stack(halves(four[order]))


def iota(shape, axis):
    return lax.broadcasted_iota(jnp.int32, shape, axis)


def dot(a, b):
    return jnp.dot(a, b, preferred_element_type=F32)


def split(x):
    high = x.astype(BF16)
    return high, (x - high.astype(F32)).astype(BF16)


def times_left(weights, x):
    high, low = split(x)
    return dot(weights, jnp.concatenate([high, low, high, low], axis=0))


def stack_quads(x):
    return jnp.concatenate([x[:, q * QUAD : (q + 1) * QUAD] for q in range(x.shape[1] // QUAD)], axis=0)


def transform_weights(left, right):
    return np.concatenate([left, right[0], right[1]], axis=0)


def times_right(x, weights):
    high, low = split(x)
    top = weights[GROUP : GROUP + QUAD]
    return dot(high, top) + (dot(low, top) + dot(high, weights[GROUP + QUAD :]))


def flag(cond):
    return jnp.where(cond, 1.0, 0.0).astype(BF16)


def numbers():
    number = (iota((GROUP, QUAD), 0) // BLOCK) * SIDE + (iota((GROUP, QUAD), 1) % GROUP) // BLOCK
    return number.astype(F32)


def listed(picks, counts):
    valid = iota(picks.shape, 0) < counts
    return jnp.where(valid, picks.astype(F32), -1.0)


def spread_lanes(picks, width, start):
    groups = picks.shape[1]
    eight = jnp.concatenate([picks, jnp.full_like(picks, -1.0)], axis=0).astype(BF16)
    member = flag(iota((groups, width), 0) == start + iota((groups, width), 1) // GROUP)
    return dot(eight, member)


def sums_of(tiles):
    sub = iota(tiles[0].shape, 0)
    for half in (4, 2, 1):
        first = sub % (2 * half) < half
        pairs = zip(tiles[:half], tiles[half:])
        tiles = [jnp.where(first, a + pltpu.roll(a, 8 - half, 0), b + pltpu.roll(b, half, 0)) for a, b in pairs]
    return tiles[0]


def send_kernel(mom_hbm, grad_hbm, picks_hbm, counts_hbm, weights_hbm, send_ref,
                mom_ref, grad_ref, picks_ref, counts_ref, weights_ref, sems):
    width = mom_ref.shape[1]
    pairs = ((picks_hbm, picks_ref), (counts_hbm, counts_ref), (weights_hbm, weights_ref),
             (mom_hbm, mom_ref), (grad_hbm, grad_ref))
    copies = [pltpu.make_async_copy(src, dst, sems.at[i]) for i, (src, dst) in enumerate(pairs)]
    for copy in copies:
        copy.start()

    row = iota((QUAD, 128), 0)
    lane = iota((QUAD, 128), 1)
    pack = flag((row // GROUP == (lane // 16) % 4) & (row % BLOCK == (lane // BLOCK) % BLOCK))
    sub = iota((8, 128), 0)
    lane = iota((8, 128), 1)
    fits = sub % BLOCK == lane % BLOCK
    early = lane < GROUP
    number = numbers()

    for copy in copies[:3]:
        copy.wait()
    picks = listed(picks_ref[...], counts_ref[...])
    groups = picks.shape[1]
    wide = spread_lanes(picks, width, 0)
    weights = weights_ref[...]

    for copy in copies[3:]:
        copy.wait()

    moment = 0.9 * mom_ref[...] + grad_ref[...].astype(F32)
    coef = times_right(stack_quads(times_left(weights[:GROUP], moment)), weights)
    parts = []
    for q in range(width // QUAD):
        quad = coef[q * GROUP : (q + 1) * GROUP]
        for k in range(KMAX):
            pick = wide[k : k + 1, q * QUAD : (q + 1) * QUAD]
            some = jnp.zeros((8, QUAD), F32)
            for b in range(GROUP // 8):
                rows = slice(b * 8, (b + 1) * 8)
                some = jnp.where(number[rows] == pick, quad[rows], some)
            parts.append(some)
    lanes = dot(jnp.concatenate(split(jnp.concatenate(parts, axis=0)), axis=0), pack)
    lanes = lanes[: lanes.shape[0] // 2] + lanes[lanes.shape[0] // 2 :]
    done = []
    for first in range(0, width // QUAD, 4):
        rows = []
        for q in (first, first + 2):
            for k in range(KMAX):
                at = (q * KMAX + k) * 8
                two = lanes[at : at + 8], lanes[at + 32 : at + 40]
                rows.append(jnp.where(fits, jnp.where(early, *two), 0.0))
        done.append(sums_of(rows))
    part = groups // 2
    both = []
    for h in range(2):
        row = jnp.concatenate([picks[k : k + 1, h * part : (h + 1) * part] for k in range(KMAX)], axis=1)
        both += [done[2 * h], done[2 * h + 1], row]
    again = jnp.concatenate(both * 4, axis=0)
    for d in range(send_ref.shape[0] // again.shape[0]):
        send_ref[d * again.shape[0] : (d + 1) * again.shape[0], :] = again


def momentum_kernel(mom_ref, grad_ref, picks_ref, counts_ref, forward_ref, inverse_ref, out_ref):
    width = mom_ref.shape[1]
    picks = listed(picks_ref[...], counts_ref[...])
    wide = spread_lanes(picks, width, pl.program_id(0) * (width // GROUP))
    forward = forward_ref[...]
    inverse = inverse_ref[...]
    number = numbers()
    moment = 0.9 * mom_ref[...] + grad_ref[...].astype(F32)
    coef = times_right(stack_quads(times_left(forward[:GROUP], moment)), forward)
    kept = []
    for q in range(width // QUAD):
        lanes = wide[:, q * QUAD : (q + 1) * QUAD]
        hit = number == lanes[:1]
        for k in range(1, KMAX):
            hit = hit | (number == lanes[k : k + 1])
        kept.append(jnp.where(hit, coef[q * GROUP : (q + 1) * GROUP], 0.0))
    back = times_right(stack_quads(times_left(inverse[:GROUP], jnp.concatenate(kept, axis=1))), inverse)
    for q in range(width // QUAD):
        cols = slice(q * QUAD, (q + 1) * QUAD)
        out_ref[:, cols] = moment[:, cols] - back[q * GROUP : (q + 1) * GROUP]


def scatter_kernel(got_ref, _, coef_ref, energy_ref, high_ref, low_ref, rows_ref, cols_ref):
    replicas = got_ref.shape[0] // ROWS
    eights = (ROWS - 1) // KMAX
    groups = eights * 8

    def slab(r):
        return got_ref[pl.ds(r, replicas, stride=ROWS), :]

    picks = slab(ROWS - 1)
    picks = jnp.concatenate([picks, picks], axis=0).T
    first = iota((groups, 128), 1) < replicas
    picks = jnp.concatenate([
        jnp.where(first, picks[k * groups : (k + 1) * groups], picks[(k + 1) * groups : (k + 2) * groups])
        for k in range(0, KMAX, 2)
    ], axis=1)
    row_block = jnp.floor(picks * (1.0 / SIDE))
    row_high = jnp.floor(row_block * 0.25)
    rows_ref[...] = row_block - 4.0 * row_high
    cols_ref[...] = row_high * SIDE + (picks - SIDE * row_block)
    for t in range(eights):
        turned = jnp.concatenate([
            jnp.concatenate([slab(t * KMAX + k), slab(t * KMAX + k + 1)], axis=0).T for k in range(0, KMAX, 2)
        ], axis=1)
        high, low = split(turned)
        high_ref[t] = high
        low_ref[t] = low

    upper = iota((8, 128), 0) < BLOCK
    early = iota((8, 128), 1) < GROUP
    block_of_row = iota((GROUP, QUAD), 0).astype(F32)

    def eight(t, energy):
        base = pl.multiple_of(t * 8, 8)
        rows8 = rows_ref[pl.ds(base, 8), :]
        cols8 = cols_ref[pl.ds(base, 8), :]
        for g in range(8):
            vals = [high_ref[t, g * 16 : (g + 1) * 16, :], low_ref[t, g * 16 : (g + 1) * 16, :]]
            row = jnp.broadcast_to(rows8[g : g + 1], (16, QUAD))
            masks = [flag(row == float(b)) for b in range(4)]
            left = jnp.concatenate([m * v for m in masks for v in vals], axis=0)
            onehot = flag(block_of_row == cols8[g : g + 1])
            right = jnp.concatenate([onehot, onehot], axis=0)
            out = lax.dot_general(left, right, (((1,), (1,)), ((), ())), preferred_element_type=F32)
            both = [out[b * 32 : b * 32 + 16] + out[b * 32 + 16 : b * 32 + 32] for b in range(4)]
            for b in range(0, 4, 2):
                for j in range(2):
                    one, two = both[b][j * 8 : j * 8 + 8], both[b + 1][j * 8 : j * 8 + 8]
                    first = jnp.where(upper, one, pltpu.roll(two, BLOCK, 0))
                    second = jnp.where(upper, pltpu.roll(one, BLOCK, 0), two)
                    coef = jnp.where(early, first, second)
                    coef_ref[pl.ds(pl.multiple_of(t * 128 + g * 16 + b * 4, 8), 8), j * 128 : (j + 1) * 128] = coef
                    energy = energy + coef * coef
        return energy

    energy = lax.fori_loop(0, eights, eight, jnp.zeros((8, 128), F32), unroll=True)
    energy = jnp.sum(energy, axis=0, keepdims=True)
    energy_ref[...] = jnp.broadcast_to(energy, energy_ref.shape)


def inverse_kernel(core_ref, own_ref, other_ref, weights_ref, update_ref, wide_ref):
    weights = weights_ref[...]
    half_lane = iota((16, 128), 1) < GROUP
    half = update_ref.shape[1] // 2
    mine = core_ref[0] * half
    for coef_ref, start in ((own_ref, mine), (other_ref, half - mine)):
        for t in range(coef_ref.shape[0] // QUAD):
            back = times_right(coef_ref[t * QUAD : (t + 1) * QUAD, :], weights)
            for pair in range(8):
                even = back[pair * 32 : pair * 32 + 16]
                odd = back[pair * 32 + 16 : pair * 32 + 32]
                lanes = slice(pair * 128, (pair + 1) * 128)
                for w in range(2):
                    e = even[:, w * 128 : (w + 1) * 128]
                    o = odd[:, w * 128 : (w + 1) * 128]
                    wide_ref[w * 32 : w * 32 + 16, lanes] = jnp.where(half_lane, e, pltpu.roll(o, GROUP, 1))
                    wide_ref[w * 32 + 16 : w * 32 + 32, lanes] = jnp.where(half_lane, pltpu.roll(e, GROUP, 1), o)
            update_ref[:, pl.ds(pl.multiple_of(start + t * 1024, 1024), 1024)] = times_left(
                weights[:GROUP], wide_ref[...])


def weights_kernel(replicas, total_rows, energy_ref, update_ref, weights_ref, out_hbm, out_ref, sems):
    mean = jnp.broadcast_to(jnp.sum(energy_ref[...]) * (1.0 / (replicas * replicas * total_rows)), (8, 128))
    factor = ((0.5 / replicas) / jnp.sqrt(mean + 1e-06))[:1, :1]
    copies = []
    part = out_ref.shape[0] // 4
    for s in range(4):
        rows = slice(s * part, (s + 1) * part)
        out_ref[rows, :] = weights_ref[rows, :] - update_ref[rows, :] * factor
        copies.append(pltpu.make_async_copy(out_ref.at[rows, :], out_hbm.at[rows, :], sems.at[s]))
        copies[-1].start()
    for copy in copies:
        copy.wait()


def whole(shape):
    return pl.BlockSpec(shape, lambda *_: (0,) * len(shape))


def on_device(momentum, grad, weights, picks, counts):
    width = weights.shape[1]
    nchunk = width // GROUP
    replicas = lax.axis_size("dp")
    nmp = lax.axis_size("mp")
    mat = basis()
    step_width = 1024
    steps = width // step_width
    half = width // 2
    tile = pl.BlockSpec((GROUP, step_width), lambda s: (0, s))
    forward = jnp.asarray(transform_weights(left_weights(mat), right_weights(mat.T)))
    inverse = jnp.asarray(transform_weights(left_weights(mat.T), right_weights(mat)))
    scatter = jnp.asarray(transform_weights(left_weights(mat.T), scatter_weights(mat)))
    hbm = pl.BlockSpec(memory_space=pltpu.HBM)
    vmem = pl.BlockSpec(memory_space=pltpu.VMEM)
    taken = [pltpu.with_memory_space_constraint(x, pltpu.HBM)
             for x in (momentum[0], grad[0], picks[0, 0].T, counts[0], forward)]
    send = pl.pallas_call(
        send_kernel,
        in_specs=[hbm] * 5,
        out_shape=jax.ShapeDtypeStruct((replicas * ROWS, 128), F32),
        scratch_shapes=[
            pltpu.VMEM((GROUP, width), F32),
            pltpu.VMEM((GROUP, width), BF16),
            pltpu.VMEM((KMAX, nchunk), jnp.int32),
            pltpu.VMEM((1, nchunk), jnp.int32),
            pltpu.VMEM(forward.shape, BF16),
            pltpu.SemaphoreType.DMA((5,)),
        ],
        compiler_params=PARAMS,
        name="send",
    )(*taken)

    got = lax.all_to_all(send.reshape(replicas * ROWS, 1, 128), "dp", 0, 0, tiled=True)
    new_momentum = pl.pallas_call(
        momentum_kernel,
        grid=(steps,),
        in_specs=[tile, tile, whole((KMAX, nchunk)), whole((1, nchunk)), whole(forward.shape), whole(inverse.shape)],
        out_specs=tile,
        out_shape=jax.ShapeDtypeStruct((GROUP, width), F32),
        compiler_params=PARAMS,
        cost_estimate=pl.CostEstimate(flops=12 * 2 * 2 * GROUP * GROUP * width, bytes_accessed=10 * GROUP * width,
                                      transcendentals=0),
        name="momentum",
    )(*taken, pltpu.with_memory_space_constraint(inverse, pltpu.HBM))
    coef, energy = pl.pallas_call(
        scatter_kernel,
        in_specs=[vmem, hbm],
        out_shape=[jax.ShapeDtypeStruct((half // 4, QUAD), F32), jax.ShapeDtypeStruct((2 * nmp, 128), F32)],
        scratch_shapes=[
            pltpu.VMEM((nchunk // 16, 128, QUAD), BF16),
            pltpu.VMEM((nchunk // 16, 128, QUAD), BF16),
            pltpu.VMEM((nchunk // 2, QUAD), F32),
            pltpu.VMEM((nchunk // 2, QUAD), F32),
        ],
        compiler_params=PARAMS,
        name="scatter",
    )(got.reshape(replicas * ROWS, 128), pltpu.with_memory_space_constraint(new_momentum, pltpu.HBM))
    partners = [[(2 * chip + core) * nmp + z for z in reversed(range(nmp)) for core in range(2)] for chip in range(replicas // 2)]
    energies = lax.all_to_all(energy.reshape(2 * nmp, 1, 128), ("dp", "mp"), 0, 0, tiled=True,
                              axis_index_groups=partners).reshape(2 * nmp, 128)
    other = lax.ppermute(coef, "dp", [(p, p ^ 1) for p in range(replicas)])
    core = jnp.bitwise_and(lax.axis_index("dp"), 1).astype(jnp.int32).reshape(1)
    update = pl.pallas_call(
        inverse_kernel,
        in_specs=[pl.BlockSpec(memory_space=pltpu.SMEM)] + [vmem] * 3,
        out_shape=jax.ShapeDtypeStruct((GROUP, width), F32),
        scratch_shapes=[pltpu.VMEM((GROUP, 1024), F32)],
        compiler_params=PARAMS,
        cost_estimate=pl.CostEstimate(flops=6 * 2 * 2 * GROUP * GROUP * width, bytes_accessed=8 * GROUP * width,
                                      transcendentals=0),
        name="inverse",
    )(core, coef, other, scatter)
    new_weights = pl.pallas_call(
        functools.partial(weights_kernel, float(replicas), float(GROUP * nmp * width)),
        in_specs=[vmem] * 3,
        out_specs=hbm,
        out_shape=jax.ShapeDtypeStruct((GROUP, width), F32),
        scratch_shapes=[pltpu.VMEM((GROUP, width), F32), pltpu.SemaphoreType.DMA((4,))],
        compiler_params=PARAMS,
        name="weights",
    )(energies, update, weights)
    return (new_momentum[None], new_weights)


def solution(mesh):
    in_specs = (
        P("dp", "mp", None),
        P("dp", "mp", None),
        P("mp", None),
        P("dp", "mp", None, None),
        P("dp", "mp", None),
    )
    out_specs = (P("dp", "mp", None), P("mp", None))
    return jax.shard_map(
        on_device, mesh=mesh, in_specs=in_specs, out_specs=out_specs, check_vma=False
    )
```

```python
import functools

import jax
import jax.numpy as jnp
import ml_dtypes
import numpy as np
from jax import lax
from jax.experimental import pallas as pl
from jax.experimental.pallas import tpu as pltpu
from jax.sharding import PartitionSpec as P

GROUP = 64
BLOCK = 4
KMAX = 4
SIDE = GROUP // BLOCK
QUAD = 4 * GROUP
ROWS = 17
F32 = jnp.float32
BF16 = jnp.bfloat16
PARAMS = pltpu.CompilerParams(vmem_limit_bytes=24 * 1024 * 1024)


def basis():
    rows = np.arange(GROUP, dtype=np.float64)[:, None]
    cols = np.arange(GROUP, dtype=np.float64)[None, :]
    waves = np.cos(np.pi * (2.0 * cols + 1.0) * rows / (2.0 * GROUP))
    factor = np.where(rows == 0.0, np.sqrt(1.0 / GROUP), np.sqrt(2.0 / GROUP))
    return (waves * factor).astype(np.float32)


def halves(mat):
    high = mat.astype(ml_dtypes.bfloat16)
    low = (mat - high.astype(np.float32)).astype(ml_dtypes.bfloat16)
    return high, low


def left_weights(mat):
    high, low = halves(mat)
    return np.concatenate([high, high, low, low], axis=1)


def right_weights(mat):
    return np.stack(halves(np.kron(np.eye(4, dtype=np.float32), mat)))


def scatter_weights(mat):
    four = np.kron(np.eye(4, dtype=np.float32), mat)
    order = np.arange(QUAD).reshape(4, SIDE, BLOCK).transpose(2, 0, 1).reshape(-1)
    return np.stack(halves(four[order]))


def iota(shape, axis):
    return lax.broadcasted_iota(jnp.int32, shape, axis)


def dot(a, b):
    return jnp.dot(a, b, preferred_element_type=F32)


def split(x):
    high = x.astype(BF16)
    return high, (x - high.astype(F32)).astype(BF16)


def times_left(weights, x):
    high, low = split(x)
    return dot(weights, jnp.concatenate([high, low, high, low], axis=0))


def stack_quads(x):
    return jnp.concatenate([x[:, q * QUAD : (q + 1) * QUAD] for q in range(x.shape[1] // QUAD)], axis=0)


def transform_weights(left, right):
    return np.concatenate([left, right[0], right[1]], axis=0)


def times_right(x, weights):
    high, low = split(x)
    top = weights[GROUP : GROUP + QUAD]
    return dot(high, top) + (dot(low, top) + dot(high, weights[GROUP + QUAD :]))


def flag(cond):
    return jnp.where(cond, 1.0, 0.0).astype(BF16)


def numbers():
    number = (iota((GROUP, QUAD), 0) // BLOCK) * SIDE + (iota((GROUP, QUAD), 1) % GROUP) // BLOCK
    return number.astype(F32)


def listed(picks, counts):
    valid = iota(picks.shape, 0) < counts
    return jnp.where(valid, picks.astype(F32), -1.0)


def spread_lanes(picks, width, start):
    groups = picks.shape[1]
    eight = jnp.concatenate([picks, jnp.full_like(picks, -1.0)], axis=0).astype(BF16)
    member = flag(iota((groups, width), 0) == start + iota((groups, width), 1) // GROUP)
    return dot(eight, member)


def sums_of(tiles):
    sub = iota(tiles[0].shape, 0)
    for half in (4, 2, 1):
        first = sub % (2 * half) < half
        pairs = zip(tiles[:half], tiles[half:])
        tiles = [jnp.where(first, a + pltpu.roll(a, 8 - half, 0), b + pltpu.roll(b, half, 0)) for a, b in pairs]
    return tiles[0]


def send_kernel(mom_hbm, grad_hbm, picks_hbm, counts_hbm, weights_hbm, send_ref,
                mom_ref, grad_ref, picks_ref, counts_ref, weights_ref, sems):
    width = mom_ref.shape[1]
    pairs = ((picks_hbm, picks_ref), (counts_hbm, counts_ref), (weights_hbm, weights_ref),
             (mom_hbm, mom_ref), (grad_hbm, grad_ref))
    copies = [pltpu.make_async_copy(src, dst, sems.at[i]) for i, (src, dst) in enumerate(pairs)]
    for copy in copies:
        copy.start()

    row = iota((QUAD, 128), 0)
    lane = iota((QUAD, 128), 1)
    pack = flag((row // GROUP == (lane // 16) % 4) & (row % BLOCK == (lane // BLOCK) % BLOCK))
    sub = iota((8, 128), 0)
    lane = iota((8, 128), 1)
    fits = sub % BLOCK == lane % BLOCK
    early = lane < GROUP
    number = numbers()

    for copy in copies[:3]:
        copy.wait()
    picks = listed(picks_ref[...], counts_ref[...])
    groups = picks.shape[1]
    wide = spread_lanes(picks, width, 0)
    weights = weights_ref[...]

    for copy in copies[3:]:
        copy.wait()

    moment = 0.9 * mom_ref[...] + grad_ref[...].astype(F32)
    coef = times_right(stack_quads(times_left(weights[:GROUP], moment)), weights)
    parts = []
    for q in range(width // QUAD):
        quad = coef[q * GROUP : (q + 1) * GROUP]
        for k in range(KMAX):
            pick = wide[k : k + 1, q * QUAD : (q + 1) * QUAD]
            some = jnp.zeros((8, QUAD), F32)
            for b in range(GROUP // 8):
                rows = slice(b * 8, (b + 1) * 8)
                some = jnp.where(number[rows] == pick, quad[rows], some)
            parts.append(some)
    lanes = dot(jnp.concatenate(split(jnp.concatenate(parts, axis=0)), axis=0), pack)
    lanes = lanes[: lanes.shape[0] // 2] + lanes[lanes.shape[0] // 2 :]
    done = []
    for first in range(0, width // QUAD, 4):
        rows = []
        for q in (first, first + 2):
            for k in range(KMAX):
                at = (q * KMAX + k) * 8
                two = lanes[at : at + 8], lanes[at + 32 : at + 40]
                rows.append(jnp.where(fits, jnp.where(early, *two), 0.0))
        done.append(sums_of(rows))
    part = groups // 2
    both = []
    for h in range(2):
        row = jnp.concatenate([picks[k : k + 1, h * part : (h + 1) * part] for k in range(KMAX)], axis=1)
        both += [done[2 * h], done[2 * h + 1], row]
    again = jnp.concatenate(both * 4, axis=0)
    for d in range(send_ref.shape[0] // again.shape[0]):
        send_ref[d * again.shape[0] : (d + 1) * again.shape[0], :] = again


def momentum_kernel(mom_ref, grad_ref, picks_ref, counts_ref, forward_ref, inverse_ref, out_ref):
    width = mom_ref.shape[1]
    picks = listed(picks_ref[...], counts_ref[...])
    wide = spread_lanes(picks, width, pl.program_id(0) * (width // GROUP))
    forward = forward_ref[...]
    inverse = inverse_ref[...]
    number = numbers()
    moment = 0.9 * mom_ref[...] + grad_ref[...].astype(F32)
    coef = times_right(stack_quads(times_left(forward[:GROUP], moment)), forward)
    kept = []
    for q in range(width // QUAD):
        lanes = wide[:, q * QUAD : (q + 1) * QUAD]
        hit = number == lanes[:1]
        for k in range(1, KMAX):
            hit = hit | (number == lanes[k : k + 1])
        kept.append(jnp.where(hit, coef[q * GROUP : (q + 1) * GROUP], 0.0))
    back = times_right(stack_quads(times_left(inverse[:GROUP], jnp.concatenate(kept, axis=1))), inverse)
    for q in range(width // QUAD):
        cols = slice(q * QUAD, (q + 1) * QUAD)
        out_ref[:, cols] = moment[:, cols] - back[q * GROUP : (q + 1) * GROUP]


def scatter_kernel(got_ref, _, coef_ref, energy_ref, high_ref, low_ref, rows_ref, cols_ref):
    replicas = got_ref.shape[0] // ROWS
    eights = (ROWS - 1) // KMAX
    groups = eights * 8

    def slab(r):
        return got_ref[pl.ds(r, replicas, stride=ROWS), :]

    picks = slab(ROWS - 1)
    picks = jnp.concatenate([picks, picks], axis=0).T
    first = iota((groups, 128), 1) < replicas
    picks = jnp.concatenate([
        jnp.where(first, picks[k * groups : (k + 1) * groups], picks[(k + 1) * groups : (k + 2) * groups])
        for k in range(0, KMAX, 2)
    ], axis=1)
    row_block = jnp.floor(picks * (1.0 / SIDE))
    row_high = jnp.floor(row_block * 0.25)
    rows_ref[...] = row_block - 4.0 * row_high
    cols_ref[...] = row_high * SIDE + (picks - SIDE * row_block)
    for t in range(eights):
        turned = jnp.concatenate([
            jnp.concatenate([slab(t * KMAX + k), slab(t * KMAX + k + 1)], axis=0).T for k in range(0, KMAX, 2)
        ], axis=1)
        high, low = split(turned)
        high_ref[t] = high
        low_ref[t] = low

    upper = iota((8, 128), 0) < BLOCK
    early = iota((8, 128), 1) < GROUP
    block_of_row = iota((GROUP, QUAD), 0).astype(F32)

    def eight(t, energy):
        base = pl.multiple_of(t * 8, 8)
        rows8 = rows_ref[pl.ds(base, 8), :]
        cols8 = cols_ref[pl.ds(base, 8), :]
        for g in range(8):
            vals = [high_ref[t, g * 16 : (g + 1) * 16, :], low_ref[t, g * 16 : (g + 1) * 16, :]]
            row = jnp.broadcast_to(rows8[g : g + 1], (16, QUAD))
            masks = [flag(row == float(b)) for b in range(4)]
            left = jnp.concatenate([m * v for m in masks for v in vals], axis=0)
            onehot = flag(block_of_row == cols8[g : g + 1])
            right = jnp.concatenate([onehot, onehot], axis=0)
            out = lax.dot_general(left, right, (((1,), (1,)), ((), ())), preferred_element_type=F32)
            both = [out[b * 32 : b * 32 + 16] + out[b * 32 + 16 : b * 32 + 32] for b in range(4)]
            for b in range(0, 4, 2):
                for j in range(2):
                    one, two = both[b][j * 8 : j * 8 + 8], both[b + 1][j * 8 : j * 8 + 8]
                    first = jnp.where(upper, one, pltpu.roll(two, BLOCK, 0))
                    second = jnp.where(upper, pltpu.roll(one, BLOCK, 0), two)
                    coef = jnp.where(early, first, second) * (1.0 / replicas)
                    coef_ref[pl.ds(pl.multiple_of(t * 128 + g * 16 + b * 4, 8), 8), j * 128 : (j + 1) * 128] = coef
                    energy = energy + coef * coef
        return energy

    energy = lax.fori_loop(0, eights, eight, jnp.zeros((8, 128), F32), unroll=True)
    energy = jnp.sum(energy, axis=0, keepdims=True)
    energy_ref[...] = jnp.broadcast_to(energy, energy_ref.shape)


def inverse_kernel(core_ref, own_ref, other_ref, weights_ref, update_ref, wide_ref):
    weights = weights_ref[...]
    half_lane = iota((16, 128), 1) < GROUP
    half = update_ref.shape[1] // 2
    mine = core_ref[0] * half
    for coef_ref, start in ((own_ref, mine), (other_ref, half - mine)):
        for t in range(coef_ref.shape[0] // QUAD):
            back = times_right(coef_ref[t * QUAD : (t + 1) * QUAD, :], weights)
            for pair in range(8):
                even = back[pair * 32 : pair * 32 + 16]
                odd = back[pair * 32 + 16 : pair * 32 + 32]
                lanes = slice(pair * 128, (pair + 1) * 128)
                for w in range(2):
                    e = even[:, w * 128 : (w + 1) * 128]
                    o = odd[:, w * 128 : (w + 1) * 128]
                    wide_ref[w * 32 : w * 32 + 16, lanes] = jnp.where(half_lane, e, pltpu.roll(o, GROUP, 1))
                    wide_ref[w * 32 + 16 : w * 32 + 32, lanes] = jnp.where(half_lane, pltpu.roll(e, GROUP, 1), o)
            update_ref[:, pl.ds(pl.multiple_of(start + t * 1024, 1024), 1024)] = times_left(
                weights[:GROUP], wide_ref[...])


def weights_kernel(elements, energy_ref, update_ref, weights_ref, out_hbm, out_ref, sems):
    mean = jnp.broadcast_to(jnp.sum(energy_ref[...]) * (1.0 / elements), (8, 128))
    factor = (0.5 / jnp.sqrt(mean + 1e-06))[:1, :1]
    copies = []
    part = out_ref.shape[0] // 4
    for s in range(4):
        rows = slice(s * part, (s + 1) * part)
        out_ref[rows, :] = weights_ref[rows, :] - update_ref[rows, :] * factor
        copies.append(pltpu.make_async_copy(out_ref.at[rows, :], out_hbm.at[rows, :], sems.at[s]))
        copies[-1].start()
    for copy in copies:
        copy.wait()


def whole(shape):
    return pl.BlockSpec(shape, lambda *_: (0,) * len(shape))


def on_device(momentum, grad, weights, picks, counts):
    width = weights.shape[1]
    nchunk = width // GROUP
    replicas = lax.axis_size("dp")
    nmp = lax.axis_size("mp")
    mat = basis()
    step_width = 1024
    steps = width // step_width
    half = width // 2
    tile = pl.BlockSpec((GROUP, step_width), lambda s: (0, s))
    forward = jnp.asarray(transform_weights(left_weights(mat), right_weights(mat.T)))
    inverse = jnp.asarray(transform_weights(left_weights(mat.T), right_weights(mat)))
    scatter = jnp.asarray(transform_weights(left_weights(mat.T), scatter_weights(mat)))
    hbm = pl.BlockSpec(memory_space=pltpu.HBM)
    vmem = pl.BlockSpec(memory_space=pltpu.VMEM)
    taken = [pltpu.with_memory_space_constraint(x, pltpu.HBM)
             for x in (momentum[0], grad[0], picks[0, 0].T, counts[0], forward)]
    send = pl.pallas_call(
        send_kernel,
        in_specs=[hbm] * 5,
        out_shape=jax.ShapeDtypeStruct((replicas * ROWS, 128), F32),
        scratch_shapes=[
            pltpu.VMEM((GROUP, width), F32),
            pltpu.VMEM((GROUP, width), BF16),
            pltpu.VMEM((KMAX, nchunk), jnp.int32),
            pltpu.VMEM((1, nchunk), jnp.int32),
            pltpu.VMEM(forward.shape, BF16),
            pltpu.SemaphoreType.DMA((5,)),
        ],
        compiler_params=PARAMS,
        name="send",
    )(*taken)

    order = [[(replicas // 2 + 4 + p) % replicas for p in range(replicas)]]
    got = lax.all_to_all(send.reshape(replicas * ROWS, 1, 128), "dp", 0, 0, tiled=True, axis_index_groups=order)
    new_momentum = pl.pallas_call(
        momentum_kernel,
        grid=(steps,),
        in_specs=[tile, tile, whole((KMAX, nchunk)), whole((1, nchunk)), whole(forward.shape), whole(inverse.shape)],
        out_specs=tile,
        out_shape=jax.ShapeDtypeStruct((GROUP, width), F32),
        compiler_params=PARAMS,
        cost_estimate=pl.CostEstimate(flops=12 * 2 * 2 * GROUP * GROUP * width, bytes_accessed=10 * GROUP * width,
                                      transcendentals=0),
        name="momentum",
    )(*taken, pltpu.with_memory_space_constraint(inverse, pltpu.HBM))
    coef, energy = pl.pallas_call(
        scatter_kernel,
        in_specs=[vmem, hbm],
        out_shape=[jax.ShapeDtypeStruct((half // 4, QUAD), F32), jax.ShapeDtypeStruct((2 * nmp, 128), F32)],
        scratch_shapes=[
            pltpu.VMEM((nchunk // 16, 128, QUAD), BF16),
            pltpu.VMEM((nchunk // 16, 128, QUAD), BF16),
            pltpu.VMEM((nchunk // 2, QUAD), F32),
            pltpu.VMEM((nchunk // 2, QUAD), F32),
        ],
        compiler_params=PARAMS,
        name="scatter",
    )(got.reshape(replicas * ROWS, 128), pltpu.with_memory_space_constraint(new_momentum, pltpu.HBM))
    partners = [[(2 * chip + core) * nmp + z for z in reversed(range(nmp)) for core in range(2)] for chip in range(replicas // 2)]
    energies = lax.all_to_all(energy.reshape(2 * nmp, 1, 128), ("dp", "mp"), 0, 0, tiled=True,
                              axis_index_groups=partners).reshape(2 * nmp, 128)
    other = lax.ppermute(coef, "dp", [(p, p ^ 1) for p in range(replicas)])
    core = jnp.bitwise_and(lax.axis_index("dp"), 1).astype(jnp.int32).reshape(1)
    update = pl.pallas_call(
        inverse_kernel,
        in_specs=[pl.BlockSpec(memory_space=pltpu.SMEM)] + [vmem] * 3,
        out_shape=jax.ShapeDtypeStruct((GROUP, width), F32),
        scratch_shapes=[pltpu.VMEM((GROUP, 1024), F32)],
        compiler_params=PARAMS,
        cost_estimate=pl.CostEstimate(flops=6 * 2 * 2 * GROUP * GROUP * width, bytes_accessed=8 * GROUP * width,
                                      transcendentals=0),
        name="inverse",
    )(core, coef, other, scatter)
    new_weights = pl.pallas_call(
        functools.partial(weights_kernel, float(GROUP * nmp * width)),
        in_specs=[vmem] * 3,
        out_specs=hbm,
        out_shape=jax.ShapeDtypeStruct((GROUP, width), F32),
        scratch_shapes=[pltpu.VMEM((GROUP, width), F32), pltpu.SemaphoreType.DMA((4,))],
        compiler_params=PARAMS,
        name="weights",
    )(energies, update, weights)
    return (new_momentum[None], new_weights)


def solution(mesh):
    in_specs = (
        P("dp", "mp", None),
        P("dp", "mp", None),
        P("mp", None),
        P("dp", "mp", None, None),
        P("dp", "mp", None),
    )
    out_specs = (P("dp", "mp", None), P("mp", None))
    return jax.shard_map(
        on_device, mesh=mesh, in_specs=in_specs, out_specs=out_specs, check_vma=False
    )
```

```python
import functools

import jax
import jax.numpy as jnp
import ml_dtypes
import numpy as np
from jax import lax
from jax.experimental import pallas as pl
from jax.experimental.pallas import tpu as pltpu
from jax.sharding import PartitionSpec as P

GROUP = 64
BLOCK = 4
KMAX = 4
SIDE = GROUP // BLOCK
QUAD = 4 * GROUP
ROWS = 17
F32 = jnp.float32
BF16 = jnp.bfloat16
PARAMS = pltpu.CompilerParams(vmem_limit_bytes=24 * 1024 * 1024)


def basis():
    rows = np.arange(GROUP, dtype=np.float64)[:, None]
    cols = np.arange(GROUP, dtype=np.float64)[None, :]
    waves = np.cos(np.pi * (2.0 * cols + 1.0) * rows / (2.0 * GROUP))
    factor = np.where(rows == 0.0, np.sqrt(1.0 / GROUP), np.sqrt(2.0 / GROUP))
    return (waves * factor).astype(np.float32)


def halves(mat):
    high = mat.astype(ml_dtypes.bfloat16)
    low = (mat - high.astype(np.float32)).astype(ml_dtypes.bfloat16)
    return high, low


def left_weights(mat):
    high, low = halves(mat)
    return np.concatenate([high, high, low, low], axis=1)


def right_weights(mat):
    return np.stack(halves(np.kron(np.eye(4, dtype=np.float32), mat)))


def scatter_weights(mat):
    four = np.kron(np.eye(4, dtype=np.float32), mat)
    order = np.arange(QUAD).reshape(4, SIDE, BLOCK).transpose(2, 0, 1).reshape(-1)
    return np.stack(halves(four[order]))


def iota(shape, axis):
    return lax.broadcasted_iota(jnp.int32, shape, axis)


def dot(a, b):
    return jnp.dot(a, b, preferred_element_type=F32)


def split(x):
    high = x.astype(BF16)
    return high, (x - high.astype(F32)).astype(BF16)


def times_left(weights, x):
    high, low = split(x)
    return dot(weights, jnp.concatenate([high, low, high, low], axis=0))


def stack_quads(x):
    return jnp.concatenate([x[:, q * QUAD : (q + 1) * QUAD] for q in range(x.shape[1] // QUAD)], axis=0)


def transform_weights(left, right):
    return np.concatenate([left, right[0], right[1]], axis=0)


def times_right(x, weights):
    high, low = split(x)
    top = weights[GROUP : GROUP + QUAD]
    return dot(high, top) + (dot(low, top) + dot(high, weights[GROUP + QUAD :]))


def flag(cond):
    return jnp.where(cond, 1.0, 0.0).astype(BF16)


def numbers():
    number = (iota((GROUP, QUAD), 0) // BLOCK) * SIDE + (iota((GROUP, QUAD), 1) % GROUP) // BLOCK
    return number.astype(F32)


def listed(picks, counts):
    valid = iota(picks.shape, 0) < counts
    return jnp.where(valid, picks.astype(F32), -1.0)


def spread_lanes(picks, width, start):
    groups = picks.shape[1]
    eight = jnp.concatenate([picks, jnp.full_like(picks, -1.0)], axis=0).astype(BF16)
    member = flag(iota((groups, width), 0) == start + iota((groups, width), 1) // GROUP)
    return dot(eight, member)


def sums_of(tiles):
    sub = iota(tiles[0].shape, 0)
    for half in (4, 2, 1):
        first = sub % (2 * half) < half
        pairs = zip(tiles[:half], tiles[half:])
        tiles = [jnp.where(first, a + pltpu.roll(a, 8 - half, 0), b + pltpu.roll(b, half, 0)) for a, b in pairs]
    return tiles[0]


def send_kernel(mom_hbm, grad_hbm, picks_hbm, counts_hbm, weights_hbm, send_ref,
                mom_ref, grad_ref, picks_ref, counts_ref, weights_ref, sems):
    width = mom_ref.shape[1]
    pairs = ((picks_hbm, picks_ref), (counts_hbm, counts_ref), (weights_hbm, weights_ref),
             (mom_hbm, mom_ref), (grad_hbm, grad_ref))
    copies = [pltpu.make_async_copy(src, dst, sems.at[i]) for i, (src, dst) in enumerate(pairs)]
    for copy in copies:
        copy.start()

    row = iota((QUAD, 128), 0)
    lane = iota((QUAD, 128), 1)
    pack = flag((row // GROUP == (lane // 16) % 4) & (row % BLOCK == (lane // BLOCK) % BLOCK))
    sub = iota((8, 128), 0)
    lane = iota((8, 128), 1)
    fits = sub % BLOCK == lane % BLOCK
    early = lane < GROUP
    number = numbers()

    for copy in copies[:3]:
        copy.wait()
    picks = listed(picks_ref[...], counts_ref[...])
    groups = picks.shape[1]
    wide = spread_lanes(picks, width, 0)
    weights = weights_ref[...]

    for copy in copies[3:]:
        copy.wait()

    moment = 0.9 * mom_ref[...] + grad_ref[...].astype(F32)
    coef = times_right(stack_quads(times_left(weights[:GROUP], moment)), weights)
    parts = []
    for q in range(width // QUAD):
        quad = coef[q * GROUP : (q + 1) * GROUP]
        for k in range(KMAX):
            pick = wide[k : k + 1, q * QUAD : (q + 1) * QUAD]
            some = jnp.zeros((8, QUAD), F32)
            for b in range(GROUP // 8):
                rows = slice(b * 8, (b + 1) * 8)
                some = jnp.where(number[rows] == pick, quad[rows], some)
            parts.append(some)
    lanes = dot(jnp.concatenate(split(jnp.concatenate(parts, axis=0)), axis=0), pack)
    lanes = lanes[: lanes.shape[0] // 2] + lanes[lanes.shape[0] // 2 :]
    done = []
    for first in range(0, width // QUAD, 4):
        rows = []
        for q in (first, first + 2):
            for k in range(KMAX):
                at = (q * KMAX + k) * 8
                two = lanes[at : at + 8], lanes[at + 32 : at + 40]
                rows.append(jnp.where(fits, jnp.where(early, *two), 0.0))
        done.append(sums_of(rows))
    part = groups // 2
    both = []
    for h in range(2):
        row = jnp.concatenate([picks[k : k + 1, h * part : (h + 1) * part] for k in range(KMAX)], axis=1)
        both += [done[2 * h], done[2 * h + 1], row]
    again = jnp.concatenate(both * 4, axis=0)
    for d in range(send_ref.shape[0] // again.shape[0]):
        send_ref[d * again.shape[0] : (d + 1) * again.shape[0], :] = again


def momentum_kernel(mom_ref, grad_ref, picks_ref, counts_ref, forward_ref, inverse_ref, out_ref):
    width = mom_ref.shape[1]
    picks = listed(picks_ref[...], counts_ref[...])
    wide = spread_lanes(picks, width, pl.program_id(0) * (width // GROUP))
    forward = forward_ref[...]
    inverse = inverse_ref[...]
    number = numbers()
    moment = 0.9 * mom_ref[...] + grad_ref[...].astype(F32)
    coef = times_right(stack_quads(times_left(forward[:GROUP], moment)), forward)
    kept = []
    for q in range(width // QUAD):
        lanes = wide[:, q * QUAD : (q + 1) * QUAD]
        hit = number == lanes[:1]
        for k in range(1, KMAX):
            hit = hit | (number == lanes[k : k + 1])
        kept.append(jnp.where(hit, coef[q * GROUP : (q + 1) * GROUP], 0.0))
    back = times_right(stack_quads(times_left(inverse[:GROUP], jnp.concatenate(kept, axis=1))), inverse)
    for q in range(width // QUAD):
        cols = slice(q * QUAD, (q + 1) * QUAD)
        out_ref[:, cols] = moment[:, cols] - back[q * GROUP : (q + 1) * GROUP]


def scatter_kernel(got_ref, _, coef_ref, energy_ref, high_ref, low_ref, rows_ref, cols_ref):
    replicas = got_ref.shape[0] // ROWS
    eights = (ROWS - 1) // KMAX
    groups = eights * 8

    def slab(r):
        return got_ref[pl.ds(r, replicas, stride=ROWS), :]

    picks = slab(ROWS - 1)
    picks = jnp.concatenate([picks, picks], axis=0).T
    first = iota((groups, 128), 1) < replicas
    picks = jnp.concatenate([
        jnp.where(first, picks[k * groups : (k + 1) * groups], picks[(k + 1) * groups : (k + 2) * groups])
        for k in range(0, KMAX, 2)
    ], axis=1)
    row_block = jnp.floor(picks * (1.0 / SIDE))
    row_high = jnp.floor(row_block * 0.25)
    rows_ref[...] = row_block - 4.0 * row_high
    cols_ref[...] = row_high * SIDE + (picks - SIDE * row_block)
    for t in range(eights):
        turned = jnp.concatenate([
            jnp.concatenate([slab(t * KMAX + k), slab(t * KMAX + k + 1)], axis=0).T for k in range(0, KMAX, 2)
        ], axis=1)
        high, low = split(turned)
        high_ref[t] = high
        low_ref[t] = low

    upper = iota((8, 128), 0) < BLOCK
    early = iota((8, 128), 1) < GROUP
    block_of_row = iota((GROUP, QUAD), 0).astype(F32)

    def eight(t, energy):
        base = pl.multiple_of(t * 8, 8)
        rows8 = rows_ref[pl.ds(base, 8), :]
        cols8 = cols_ref[pl.ds(base, 8), :]
        for g in range(8):
            vals = [high_ref[t, g * 16 : (g + 1) * 16, :], low_ref[t, g * 16 : (g + 1) * 16, :]]
            row = jnp.broadcast_to(rows8[g : g + 1], (16, QUAD))
            masks = [flag(row == float(b)) for b in range(4)]
            left = jnp.concatenate([m * v for m in masks for v in vals], axis=0)
            onehot = flag(block_of_row == cols8[g : g + 1])
            right = jnp.concatenate([onehot, onehot], axis=0)
            out = lax.dot_general(left, right, (((1,), (1,)), ((), ())), preferred_element_type=F32)
            both = [out[b * 32 : b * 32 + 16] + out[b * 32 + 16 : b * 32 + 32] for b in range(4)]
            for b in range(0, 4, 2):
                for j in range(2):
                    one, two = both[b][j * 8 : j * 8 + 8], both[b + 1][j * 8 : j * 8 + 8]
                    first = jnp.where(upper, one, pltpu.roll(two, BLOCK, 0))
                    second = jnp.where(upper, pltpu.roll(one, BLOCK, 0), two)
                    coef = jnp.where(early, first, second) * (1.0 / replicas)
                    coef_ref[pl.ds(pl.multiple_of(t * 128 + g * 16 + b * 4, 8), 8), j * 128 : (j + 1) * 128] = coef
                    energy = energy + coef * coef
        return energy

    energy = lax.fori_loop(0, eights, eight, jnp.zeros((8, 128), F32), unroll=True)
    energy = jnp.sum(energy, axis=0, keepdims=True)
    energy_ref[...] = jnp.broadcast_to(energy, energy_ref.shape)


def inverse_kernel(core_ref, own_ref, other_ref, weights_ref, update_ref, wide_ref):
    weights = weights_ref[...]
    half_lane = iota((16, 128), 1) < GROUP
    half = update_ref.shape[1] // 2
    mine = core_ref[0] * half
    for coef_ref, start in ((own_ref, mine), (other_ref, half - mine)):
        for t in range(coef_ref.shape[0] // QUAD):
            back = times_right(coef_ref[t * QUAD : (t + 1) * QUAD, :], weights)
            for pair in range(8):
                even = back[pair * 32 : pair * 32 + 16]
                odd = back[pair * 32 + 16 : pair * 32 + 32]
                lanes = slice(pair * 128, (pair + 1) * 128)
                for w in range(2):
                    e = even[:, w * 128 : (w + 1) * 128]
                    o = odd[:, w * 128 : (w + 1) * 128]
                    wide_ref[w * 32 : w * 32 + 16, lanes] = jnp.where(half_lane, e, pltpu.roll(o, GROUP, 1))
                    wide_ref[w * 32 + 16 : w * 32 + 32, lanes] = jnp.where(half_lane, pltpu.roll(e, GROUP, 1), o)
            update_ref[:, pl.ds(pl.multiple_of(start + t * 1024, 1024), 1024)] = times_left(
                weights[:GROUP], wide_ref[...])


def weights_kernel(elements, energy_ref, update_ref, weights_ref, out_hbm, out_ref, sems):
    mean = jnp.broadcast_to(jnp.sum(energy_ref[...]) * (1.0 / elements), (8, 128))
    factor = (0.5 / jnp.sqrt(mean + 1e-06))[:1, :1]
    copies = []
    part = out_ref.shape[0] // 4
    for s in range(4):
        rows = slice(s * part, (s + 1) * part)
        out_ref[rows, :] = weights_ref[rows, :] - update_ref[rows, :] * factor
        copies.append(pltpu.make_async_copy(out_ref.at[rows, :], out_hbm.at[rows, :], sems.at[s]))
        copies[-1].start()
    for copy in copies:
        copy.wait()


def whole(shape):
    return pl.BlockSpec(shape, lambda *_: (0,) * len(shape))


def on_device(momentum, grad, weights, picks, counts):
    width = weights.shape[1]
    nchunk = width // GROUP
    replicas = lax.axis_size("dp")
    nmp = lax.axis_size("mp")
    mat = basis()
    step_width = 1024
    steps = width // step_width
    half = width // 2
    tile = pl.BlockSpec((GROUP, step_width), lambda s: (0, s))
    forward = jnp.asarray(transform_weights(left_weights(mat), right_weights(mat.T)))
    inverse = jnp.asarray(transform_weights(left_weights(mat.T), right_weights(mat)))
    scatter = jnp.asarray(transform_weights(left_weights(mat.T), scatter_weights(mat)))
    hbm = pl.BlockSpec(memory_space=pltpu.HBM)
    vmem = pl.BlockSpec(memory_space=pltpu.VMEM)
    taken = [pltpu.with_memory_space_constraint(x, pltpu.HBM)
             for x in (momentum[0], grad[0], picks[0, 0].T, counts[0], forward)]
    send = pl.pallas_call(
        send_kernel,
        in_specs=[hbm] * 5,
        out_shape=jax.ShapeDtypeStruct((replicas * ROWS, 128), F32),
        scratch_shapes=[
            pltpu.VMEM((GROUP, width), F32),
            pltpu.VMEM((GROUP, width), BF16),
            pltpu.VMEM((KMAX, nchunk), jnp.int32),
            pltpu.VMEM((1, nchunk), jnp.int32),
            pltpu.VMEM(forward.shape, BF16),
            pltpu.SemaphoreType.DMA((5,)),
        ],
        compiler_params=PARAMS,
        name="send",
    )(*taken)

    order = [[(replicas // 2 + 4 + 37 * p) % replicas for p in range(replicas)]]
    got = lax.all_to_all(send.reshape(replicas * ROWS, 1, 128), "dp", 0, 0, tiled=True, axis_index_groups=order)
    new_momentum = pl.pallas_call(
        momentum_kernel,
        grid=(steps,),
        in_specs=[tile, tile, whole((KMAX, nchunk)), whole((1, nchunk)), whole(forward.shape), whole(inverse.shape)],
        out_specs=tile,
        out_shape=jax.ShapeDtypeStruct((GROUP, width), F32),
        compiler_params=PARAMS,
        cost_estimate=pl.CostEstimate(flops=12 * 2 * 2 * GROUP * GROUP * width, bytes_accessed=10 * GROUP * width,
                                      transcendentals=0),
        name="momentum",
    )(*taken, pltpu.with_memory_space_constraint(inverse, pltpu.HBM))
    coef, energy = pl.pallas_call(
        scatter_kernel,
        in_specs=[vmem, hbm],
        out_shape=[jax.ShapeDtypeStruct((half // 4, QUAD), F32), jax.ShapeDtypeStruct((2 * nmp, 128), F32)],
        scratch_shapes=[
            pltpu.VMEM((nchunk // 16, 128, QUAD), BF16),
            pltpu.VMEM((nchunk // 16, 128, QUAD), BF16),
            pltpu.VMEM((nchunk // 2, QUAD), F32),
            pltpu.VMEM((nchunk // 2, QUAD), F32),
        ],
        compiler_params=PARAMS,
        name="scatter",
    )(got.reshape(replicas * ROWS, 128), pltpu.with_memory_space_constraint(new_momentum, pltpu.HBM))
    partners = [[(2 * chip + core) * nmp + z for z in reversed(range(nmp)) for core in range(2)] for chip in range(replicas // 2)]
    energies = lax.all_to_all(energy.reshape(2 * nmp, 1, 128), ("dp", "mp"), 0, 0, tiled=True,
                              axis_index_groups=partners).reshape(2 * nmp, 128)
    other = lax.ppermute(coef, "dp", [(p, p ^ 1) for p in range(replicas)])
    core = jnp.bitwise_and(lax.axis_index("dp"), 1).astype(jnp.int32).reshape(1)
    update = pl.pallas_call(
        inverse_kernel,
        in_specs=[pl.BlockSpec(memory_space=pltpu.SMEM)] + [vmem] * 3,
        out_shape=jax.ShapeDtypeStruct((GROUP, width), F32),
        scratch_shapes=[pltpu.VMEM((GROUP, 1024), F32)],
        compiler_params=PARAMS,
        cost_estimate=pl.CostEstimate(flops=6 * 2 * 2 * GROUP * GROUP * width, bytes_accessed=8 * GROUP * width,
                                      transcendentals=0),
        name="inverse",
    )(core, coef, other, scatter)
    new_weights = pl.pallas_call(
        functools.partial(weights_kernel, float(GROUP * nmp * width)),
        in_specs=[vmem] * 3,
        out_specs=hbm,
        out_shape=jax.ShapeDtypeStruct((GROUP, width), F32),
        scratch_shapes=[pltpu.VMEM((GROUP, width), F32), pltpu.SemaphoreType.DMA((4,))],
        compiler_params=PARAMS,
        name="weights",
    )(energies, update, weights)
    return (new_momentum[None], new_weights)


def solution(mesh):
    in_specs = (
        P("dp", "mp", None),
        P("dp", "mp", None),
        P("mp", None),
        P("dp", "mp", None, None),
        P("dp", "mp", None),
    )
    out_specs = (P("dp", "mp", None), P("mp", None))
    return jax.shard_map(
        on_device, mesh=mesh, in_specs=in_specs, out_specs=out_specs, check_vma=False
    )
```

```python
import functools

import jax
import jax.numpy as jnp
import ml_dtypes
import numpy as np
from jax import lax
from jax.experimental import pallas as pl
from jax.experimental.pallas import tpu as pltpu
from jax.sharding import PartitionSpec as P

GROUP = 64
BLOCK = 4
KMAX = 4
SIDE = GROUP // BLOCK
QUAD = 4 * GROUP
ROWS = 17
F32 = jnp.float32
BF16 = jnp.bfloat16
PARAMS = pltpu.CompilerParams(vmem_limit_bytes=24 * 1024 * 1024)


def basis():
    rows = np.arange(GROUP, dtype=np.float64)[:, None]
    cols = np.arange(GROUP, dtype=np.float64)[None, :]
    waves = np.cos(np.pi * (2.0 * cols + 1.0) * rows / (2.0 * GROUP))
    factor = np.where(rows == 0.0, np.sqrt(1.0 / GROUP), np.sqrt(2.0 / GROUP))
    return (waves * factor).astype(np.float32)


def halves(mat):
    high = mat.astype(ml_dtypes.bfloat16)
    low = (mat - high.astype(np.float32)).astype(ml_dtypes.bfloat16)
    return high, low


def left_weights(mat):
    high, low = halves(mat)
    return np.concatenate([high, high, low, low], axis=1)


def right_weights(mat):
    return np.stack(halves(np.kron(np.eye(4, dtype=np.float32), mat)))


def scatter_weights(mat):
    four = np.kron(np.eye(4, dtype=np.float32), mat)
    order = np.arange(QUAD).reshape(4, SIDE, BLOCK).transpose(2, 0, 1).reshape(-1)
    return np.stack(halves(four[order]))


def iota(shape, axis):
    return lax.broadcasted_iota(jnp.int32, shape, axis)


def dot(a, b):
    return jnp.dot(a, b, preferred_element_type=F32)


def split(x):
    high = x.astype(BF16)
    return high, (x - high.astype(F32)).astype(BF16)


def times_left(weights, x):
    high, low = split(x)
    return dot(weights[:, : 3 * GROUP], jnp.concatenate([high, low, high], axis=0))


def stack_quads(x):
    return jnp.concatenate([x[:, q * QUAD : (q + 1) * QUAD] for q in range(x.shape[1] // QUAD)], axis=0)


def transform_weights(left, right):
    return np.concatenate([left, right[0], right[1]], axis=0)


def times_right(x, weights):
    high, low = split(x)
    top = weights[GROUP : GROUP + QUAD]
    return dot(high, top) + (dot(low, top) + dot(high, weights[GROUP + QUAD :]))


def flag(cond):
    return jnp.where(cond, 1.0, 0.0).astype(BF16)


def numbers():
    number = (iota((GROUP, QUAD), 0) // BLOCK) * SIDE + (iota((GROUP, QUAD), 1) % GROUP) // BLOCK
    return number.astype(F32)


def listed(picks, counts):
    valid = iota(picks.shape, 0) < counts
    return jnp.where(valid, picks.astype(F32), -1.0)


def spread_lanes(picks, width, start):
    groups = picks.shape[1]
    eight = jnp.concatenate([picks, jnp.full_like(picks, -1.0)], axis=0).astype(BF16)
    member = flag(iota((groups, width), 0) == start + iota((groups, width), 1) // GROUP)
    return dot(eight, member)


def sums_of(tiles):
    sub = iota(tiles[0].shape, 0)
    for half in (4, 2, 1):
        first = sub % (2 * half) < half
        pairs = zip(tiles[:half], tiles[half:])
        tiles = [jnp.where(first, a + pltpu.roll(a, 8 - half, 0), b + pltpu.roll(b, half, 0)) for a, b in pairs]
    return tiles[0]


def send_kernel(mom_hbm, grad_hbm, picks_hbm, counts_hbm, weights_hbm, send_ref,
                mom_ref, grad_ref, picks_ref, counts_ref, weights_ref, sems):
    width = mom_ref.shape[1]
    pairs = ((picks_hbm, picks_ref), (counts_hbm, counts_ref), (weights_hbm, weights_ref),
             (mom_hbm, mom_ref), (grad_hbm, grad_ref))
    copies = [pltpu.make_async_copy(src, dst, sems.at[i]) for i, (src, dst) in enumerate(pairs)]
    for copy in copies:
        copy.start()

    row = iota((QUAD, 128), 0)
    lane = iota((QUAD, 128), 1)
    pack = flag((row // GROUP == (lane // 16) % 4) & (row % BLOCK == (lane // BLOCK) % BLOCK))
    sub = iota((8, 128), 0)
    lane = iota((8, 128), 1)
    fits = sub % BLOCK == lane % BLOCK
    early = lane < GROUP
    number = numbers()

    for copy in copies[:3]:
        copy.wait()
    picks = listed(picks_ref[...], counts_ref[...])
    groups = picks.shape[1]
    wide = spread_lanes(picks, width, 0)
    weights = weights_ref[...]

    for copy in copies[3:]:
        copy.wait()

    moment = 0.9 * mom_ref[...] + grad_ref[...].astype(F32)
    coef = times_right(stack_quads(times_left(weights[:GROUP], moment)), weights)
    parts = []
    for q in range(width // QUAD):
        quad = coef[q * GROUP : (q + 1) * GROUP]
        for k in range(KMAX):
            pick = wide[k : k + 1, q * QUAD : (q + 1) * QUAD]
            some = jnp.zeros((8, QUAD), F32)
            for b in range(GROUP // 8):
                rows = slice(b * 8, (b + 1) * 8)
                some = jnp.where(number[rows] == pick, quad[rows], some)
            parts.append(some)
    lanes = dot(jnp.concatenate(split(jnp.concatenate(parts, axis=0)), axis=0), pack)
    lanes = lanes[: lanes.shape[0] // 2] + lanes[lanes.shape[0] // 2 :]
    done = []
    for first in range(0, width // QUAD, 4):
        rows = []
        for q in (first, first + 2):
            for k in range(KMAX):
                at = (q * KMAX + k) * 8
                two = lanes[at : at + 8], lanes[at + 32 : at + 40]
                rows.append(jnp.where(fits, jnp.where(early, *two), 0.0))
        done.append(sums_of(rows))
    part = groups // 2
    both = []
    for h in range(2):
        row = jnp.concatenate([picks[k : k + 1, h * part : (h + 1) * part] for k in range(KMAX)], axis=1)
        both += [done[2 * h], done[2 * h + 1], row]
    again = jnp.concatenate(both * 4, axis=0)
    for d in range(send_ref.shape[0] // again.shape[0]):
        send_ref[d * again.shape[0] : (d + 1) * again.shape[0], :] = again


def momentum_kernel(mom_ref, grad_ref, picks_ref, counts_ref, forward_ref, inverse_ref, out_ref):
    width = mom_ref.shape[1]
    picks = listed(picks_ref[...], counts_ref[...])
    wide = spread_lanes(picks, width, pl.program_id(0) * (width // GROUP))
    forward = forward_ref[...]
    inverse = inverse_ref[...]
    number = numbers()
    moment = 0.9 * mom_ref[...] + grad_ref[...].astype(F32)
    coef = times_right(stack_quads(times_left(forward[:GROUP], moment)), forward)
    kept = []
    for q in range(width // QUAD):
        lanes = wide[:, q * QUAD : (q + 1) * QUAD]
        hit = number == lanes[:1]
        for k in range(1, KMAX):
            hit = hit | (number == lanes[k : k + 1])
        kept.append(jnp.where(hit, coef[q * GROUP : (q + 1) * GROUP], 0.0))
    back = times_right(stack_quads(times_left(inverse[:GROUP], jnp.concatenate(kept, axis=1))), inverse)
    for q in range(width // QUAD):
        cols = slice(q * QUAD, (q + 1) * QUAD)
        out_ref[:, cols] = moment[:, cols] - back[q * GROUP : (q + 1) * GROUP]


def scatter_kernel(got_ref, _, coef_ref, energy_ref, high_ref, low_ref, rows_ref, cols_ref):
    replicas = got_ref.shape[0] // ROWS
    eights = (ROWS - 1) // KMAX
    groups = eights * 8

    def slab(r):
        return got_ref[pl.ds(r, replicas, stride=ROWS), :]

    picks = slab(ROWS - 1)
    picks = jnp.concatenate([picks, picks], axis=0).T
    first = iota((groups, 128), 1) < replicas
    picks = jnp.concatenate([
        jnp.where(first, picks[k * groups : (k + 1) * groups], picks[(k + 1) * groups : (k + 2) * groups])
        for k in range(0, KMAX, 2)
    ], axis=1)
    row_block = jnp.floor(picks * (1.0 / SIDE))
    row_high = jnp.floor(row_block * 0.25)
    rows_ref[...] = row_block - 4.0 * row_high
    cols_ref[...] = row_high * SIDE + (picks - SIDE * row_block)
    for t in range(eights):
        turned = jnp.concatenate([
            jnp.concatenate([slab(t * KMAX + k), slab(t * KMAX + k + 1)], axis=0).T for k in range(0, KMAX, 2)
        ], axis=1)
        high, low = split(turned)
        high_ref[t] = high
        low_ref[t] = low

    upper = iota((8, 128), 0) < BLOCK
    early = iota((8, 128), 1) < GROUP
    block_of_row = iota((GROUP, QUAD), 0).astype(F32)

    def eight(t, energy):
        base = pl.multiple_of(t * 8, 8)
        rows8 = rows_ref[pl.ds(base, 8), :]
        cols8 = cols_ref[pl.ds(base, 8), :]
        for g in range(8):
            vals = [high_ref[t, g * 16 : (g + 1) * 16, :], low_ref[t, g * 16 : (g + 1) * 16, :]]
            row = jnp.broadcast_to(rows8[g : g + 1], (16, QUAD))
            masks = [flag(row == float(b)) for b in range(4)]
            left = jnp.concatenate([m * v for m in masks for v in vals], axis=0)
            onehot = flag(block_of_row == cols8[g : g + 1])
            right = jnp.concatenate([onehot, onehot], axis=0)
            out = lax.dot_general(left, right, (((1,), (1,)), ((), ())), preferred_element_type=F32)
            both = [out[b * 32 : b * 32 + 16] + out[b * 32 + 16 : b * 32 + 32] for b in range(4)]
            for b in range(0, 4, 2):
                for j in range(2):
                    one, two = both[b][j * 8 : j * 8 + 8], both[b + 1][j * 8 : j * 8 + 8]
                    first = jnp.where(upper, one, pltpu.roll(two, BLOCK, 0))
                    second = jnp.where(upper, pltpu.roll(one, BLOCK, 0), two)
                    coef = jnp.where(early, first, second) * (1.0 / replicas)
                    coef_ref[pl.ds(pl.multiple_of(t * 128 + g * 16 + b * 4, 8), 8), j * 128 : (j + 1) * 128] = coef
                    energy = energy + coef * coef
        return energy

    energy = lax.fori_loop(0, eights, eight, jnp.zeros((8, 128), F32), unroll=True)
    energy = jnp.sum(energy, axis=0, keepdims=True)
    energy_ref[...] = jnp.broadcast_to(energy, energy_ref.shape)


def inverse_kernel(core_ref, own_ref, other_ref, weights_ref, update_ref, wide_ref):
    weights = weights_ref[...]
    half_lane = iota((16, 128), 1) < GROUP
    half = update_ref.shape[1] // 2
    mine = core_ref[0] * half
    for coef_ref, start in ((own_ref, mine), (other_ref, half - mine)):
        for t in range(coef_ref.shape[0] // QUAD):
            back = times_right(coef_ref[t * QUAD : (t + 1) * QUAD, :], weights)
            for pair in range(8):
                even = back[pair * 32 : pair * 32 + 16]
                odd = back[pair * 32 + 16 : pair * 32 + 32]
                lanes = slice(pair * 128, (pair + 1) * 128)
                for w in range(2):
                    e = even[:, w * 128 : (w + 1) * 128]
                    o = odd[:, w * 128 : (w + 1) * 128]
                    wide_ref[w * 32 : w * 32 + 16, lanes] = jnp.where(half_lane, e, pltpu.roll(o, GROUP, 1))
                    wide_ref[w * 32 + 16 : w * 32 + 32, lanes] = jnp.where(half_lane, pltpu.roll(e, GROUP, 1), o)
            update_ref[:, pl.ds(pl.multiple_of(start + t * 1024, 1024), 1024)] = times_left(
                weights[:GROUP], wide_ref[...])


def weights_kernel(elements, energy_ref, update_ref, weights_ref, out_hbm, out_ref, sems):
    mean = jnp.broadcast_to(jnp.sum(energy_ref[...]) * (1.0 / elements), (8, 128))
    factor = (0.5 / jnp.sqrt(mean + 1e-06))[:1, :1]
    copies = []
    part = out_ref.shape[0] // 8
    for s in range(8):
        rows = slice(s * part, (s + 1) * part)
        out_ref[rows, :] = weights_ref[rows, :] - update_ref[rows, :] * factor
        copies.append(pltpu.make_async_copy(out_ref.at[rows, :], out_hbm.at[rows, :], sems.at[s]))
        copies[-1].start()
    for copy in copies:
        copy.wait()


def whole(shape):
    return pl.BlockSpec(shape, lambda *_: (0,) * len(shape))


def on_device(momentum, grad, weights, picks, counts):
    width = weights.shape[1]
    nchunk = width // GROUP
    replicas = lax.axis_size("dp")
    nmp = lax.axis_size("mp")
    mat = basis()
    step_width = 1024
    steps = width // step_width
    half = width // 2
    tile = pl.BlockSpec((GROUP, step_width), lambda s: (0, s))
    forward = jnp.asarray(transform_weights(left_weights(mat), right_weights(mat.T)))
    inverse = jnp.asarray(transform_weights(left_weights(mat.T), right_weights(mat)))
    scatter = jnp.asarray(transform_weights(left_weights(mat.T), scatter_weights(mat)))
    hbm = pl.BlockSpec(memory_space=pltpu.HBM)
    vmem = pl.BlockSpec(memory_space=pltpu.VMEM)
    taken = [pltpu.with_memory_space_constraint(x, pltpu.HBM)
             for x in (momentum[0], grad[0], picks[0, 0].T, counts[0], forward)]
    send = pl.pallas_call(
        send_kernel,
        in_specs=[hbm] * 5,
        out_shape=jax.ShapeDtypeStruct((replicas * ROWS, 128), F32),
        scratch_shapes=[
            pltpu.VMEM((GROUP, width), F32),
            pltpu.VMEM((GROUP, width), BF16),
            pltpu.VMEM((KMAX, nchunk), jnp.int32),
            pltpu.VMEM((1, nchunk), jnp.int32),
            pltpu.VMEM(forward.shape, BF16),
            pltpu.SemaphoreType.DMA((5,)),
        ],
        compiler_params=PARAMS,
        name="send",
    )(*taken)

    order = [[(replicas // 2 + 4 + 37 * p) % replicas for p in range(replicas)]]
    got = lax.all_to_all(send.reshape(replicas * ROWS, 1, 128), "dp", 0, 0, tiled=True, axis_index_groups=order)
    new_momentum = pl.pallas_call(
        momentum_kernel,
        grid=(steps,),
        in_specs=[tile, tile, whole((KMAX, nchunk)), whole((1, nchunk)), whole(forward.shape), whole(inverse.shape)],
        out_specs=tile,
        out_shape=jax.ShapeDtypeStruct((GROUP, width), F32),
        compiler_params=PARAMS,
        cost_estimate=pl.CostEstimate(flops=12 * 2 * 2 * GROUP * GROUP * width, bytes_accessed=10 * GROUP * width,
                                      transcendentals=0),
        name="momentum",
    )(*taken, pltpu.with_memory_space_constraint(inverse, pltpu.HBM))
    coef, energy = pl.pallas_call(
        scatter_kernel,
        in_specs=[vmem, hbm],
        out_shape=[jax.ShapeDtypeStruct((half // 4, QUAD), F32), jax.ShapeDtypeStruct((2 * nmp, 128), F32)],
        scratch_shapes=[
            pltpu.VMEM((nchunk // 16, 128, QUAD), BF16),
            pltpu.VMEM((nchunk // 16, 128, QUAD), BF16),
            pltpu.VMEM((nchunk // 2, QUAD), F32),
            pltpu.VMEM((nchunk // 2, QUAD), F32),
        ],
        compiler_params=PARAMS,
        name="scatter",
    )(got.reshape(replicas * ROWS, 128), pltpu.with_memory_space_constraint(new_momentum, pltpu.HBM))
    partners = [[(2 * chip + core) * nmp + z for z in reversed(range(nmp)) for core in range(2)] for chip in range(replicas // 2)]
    energies = lax.all_to_all(energy.reshape(2 * nmp, 1, 128), ("dp", "mp"), 0, 0, tiled=True,
                              axis_index_groups=partners).reshape(2 * nmp, 128)
    other = lax.ppermute(coef, "dp", [(p, p ^ 1) for p in range(replicas)])
    core = jnp.bitwise_and(lax.axis_index("dp"), 1).astype(jnp.int32).reshape(1)
    update = pl.pallas_call(
        inverse_kernel,
        in_specs=[pl.BlockSpec(memory_space=pltpu.SMEM)] + [vmem] * 3,
        out_shape=jax.ShapeDtypeStruct((GROUP, width), F32),
        scratch_shapes=[pltpu.VMEM((GROUP, 1024), F32)],
        compiler_params=PARAMS,
        cost_estimate=pl.CostEstimate(flops=6 * 2 * 2 * GROUP * GROUP * width, bytes_accessed=8 * GROUP * width,
                                      transcendentals=0),
        name="inverse",
    )(core, coef, other, scatter)
    new_weights = pl.pallas_call(
        functools.partial(weights_kernel, float(GROUP * nmp * width)),
        in_specs=[vmem] * 3,
        out_specs=hbm,
        out_shape=jax.ShapeDtypeStruct((GROUP, width), F32),
        scratch_shapes=[pltpu.VMEM((GROUP, width), F32), pltpu.SemaphoreType.DMA((8,))],
        compiler_params=PARAMS,
        name="weights",
    )(energies, update, weights)
    return (new_momentum[None], new_weights)


def solution(mesh):
    in_specs = (
        P("dp", "mp", None),
        P("dp", "mp", None),
        P("mp", None),
        P("dp", "mp", None, None),
        P("dp", "mp", None),
    )
    out_specs = (P("dp", "mp", None), P("mp", None))
    return jax.shard_map(
        on_device, mesh=mesh, in_specs=in_specs, out_specs=out_specs, check_vma=False
    )
```

```python
import functools

import jax
import jax.numpy as jnp
import ml_dtypes
import numpy as np
from jax import lax
from jax.experimental import pallas as pl
from jax.experimental.pallas import tpu as pltpu
from jax.sharding import PartitionSpec as P

GROUP = 64
BLOCK = 4
KMAX = 4
SIDE = GROUP // BLOCK
QUAD = 4 * GROUP
ROWS = 17
F32 = jnp.float32
BF16 = jnp.bfloat16
PARAMS = pltpu.CompilerParams(vmem_limit_bytes=24 * 1024 * 1024)


def basis():
    rows = np.arange(GROUP, dtype=np.float64)[:, None]
    cols = np.arange(GROUP, dtype=np.float64)[None, :]
    waves = np.cos(np.pi * (2.0 * cols + 1.0) * rows / (2.0 * GROUP))
    factor = np.where(rows == 0.0, np.sqrt(1.0 / GROUP), np.sqrt(2.0 / GROUP))
    return (waves * factor).astype(np.float32)


def halves(mat):
    high = mat.astype(ml_dtypes.bfloat16)
    low = (mat - high.astype(np.float32)).astype(ml_dtypes.bfloat16)
    return high, low


def left_weights(mat):
    high, low = halves(mat)
    return np.concatenate([high, high, low, low], axis=1)


def right_weights(mat):
    return np.stack(halves(np.kron(np.eye(4, dtype=np.float32), mat)))


def scatter_weights(mat):
    four = np.kron(np.eye(4, dtype=np.float32), mat)
    order = np.arange(QUAD).reshape(4, SIDE, BLOCK).transpose(2, 0, 1).reshape(-1)
    return np.stack(halves(four[order]))


def iota(shape, axis):
    return lax.broadcasted_iota(jnp.int32, shape, axis)


def dot(a, b):
    return jnp.dot(a, b, preferred_element_type=F32)


def split(x):
    high = x.astype(BF16)
    return high, (x - high.astype(F32)).astype(BF16)


def times_left(weights, x):
    high, low = split(x)
    return dot(weights[:, : 3 * GROUP], jnp.concatenate([high, low, high], axis=0))


def stack_quads(x):
    return jnp.concatenate([x[:, q * QUAD : (q + 1) * QUAD] for q in range(x.shape[1] // QUAD)], axis=0)


def transform_weights(left, right):
    return np.concatenate([left, right[0], right[1]], axis=0)


def times_right(x, weights):
    high, low = split(x)
    top = weights[GROUP : GROUP + QUAD]
    both = dot(jnp.concatenate([high, low], axis=0), top)
    return both[: x.shape[0]] + (both[x.shape[0] :] + dot(high, weights[GROUP + QUAD :]))


def flag(cond):
    return jnp.where(cond, 1.0, 0.0).astype(BF16)


def numbers():
    number = (iota((GROUP, QUAD), 0) // BLOCK) * SIDE + (iota((GROUP, QUAD), 1) % GROUP) // BLOCK
    return number.astype(F32)


def listed(picks, counts):
    valid = iota(picks.shape, 0) < counts
    return jnp.where(valid, picks.astype(F32), -1.0)


def spread_lanes(picks, width, start):
    groups = picks.shape[1]
    eight = jnp.concatenate([picks, jnp.full_like(picks, -1.0)], axis=0).astype(BF16)
    member = flag(iota((groups, width), 0) == start + iota((groups, width), 1) // GROUP)
    return dot(eight, member)


def sums_of(tiles):
    sub = iota(tiles[0].shape, 0)
    for half in (4, 2, 1):
        first = sub % (2 * half) < half
        pairs = zip(tiles[:half], tiles[half:])
        tiles = [jnp.where(first, a + pltpu.roll(a, 8 - half, 0), b + pltpu.roll(b, half, 0)) for a, b in pairs]
    return tiles[0]


def send_kernel(mom_hbm, grad_hbm, picks_hbm, counts_hbm, weights_hbm, send_ref,
                mom_ref, grad_ref, picks_ref, counts_ref, weights_ref, sems):
    width = mom_ref.shape[1]
    pairs = ((picks_hbm, picks_ref), (counts_hbm, counts_ref), (weights_hbm, weights_ref),
             (mom_hbm, mom_ref), (grad_hbm, grad_ref))
    copies = [pltpu.make_async_copy(src, dst, sems.at[i]) for i, (src, dst) in enumerate(pairs)]
    for copy in copies:
        copy.start()

    row = iota((QUAD, 128), 0)
    lane = iota((QUAD, 128), 1)
    pack = flag((row // GROUP == (lane // 16) % 4) & (row % BLOCK == (lane // BLOCK) % BLOCK))
    sub = iota((8, 128), 0)
    lane = iota((8, 128), 1)
    fits = sub % BLOCK == lane % BLOCK
    early = lane < GROUP
    number = numbers()

    for copy in copies[:3]:
        copy.wait()
    picks = listed(picks_ref[...], counts_ref[...])
    groups = picks.shape[1]
    wide = spread_lanes(picks, width, 0)
    weights = weights_ref[...]

    for copy in copies[3:]:
        copy.wait()

    moment = 0.9 * mom_ref[...] + grad_ref[...].astype(F32)
    coef = times_right(stack_quads(times_left(weights[:GROUP], moment)), weights)
    parts = []
    for q in range(width // QUAD):
        quad = coef[q * GROUP : (q + 1) * GROUP]
        for k in range(KMAX):
            pick = wide[k : k + 1, q * QUAD : (q + 1) * QUAD]
            some = jnp.zeros((8, QUAD), F32)
            for b in range(GROUP // 8):
                rows = slice(b * 8, (b + 1) * 8)
                some = jnp.where(number[rows] == pick, quad[rows], some)
            parts.append(some)
    lanes = dot(jnp.concatenate(split(jnp.concatenate(parts, axis=0)), axis=0), pack)
    lanes = lanes[: lanes.shape[0] // 2] + lanes[lanes.shape[0] // 2 :]
    done = []
    for first in range(0, width // QUAD, 4):
        rows = []
        for q in (first, first + 2):
            for k in range(KMAX):
                at = (q * KMAX + k) * 8
                two = lanes[at : at + 8], lanes[at + 32 : at + 40]
                rows.append(jnp.where(fits, jnp.where(early, *two), 0.0))
        done.append(sums_of(rows))
    part = groups // 2
    both = []
    for h in range(2):
        row = jnp.concatenate([picks[k : k + 1, h * part : (h + 1) * part] for k in range(KMAX)], axis=1)
        both += [done[2 * h], done[2 * h + 1], row]
    again = jnp.concatenate(both * 4, axis=0)
    for d in range(send_ref.shape[0] // again.shape[0]):
        send_ref[d * again.shape[0] : (d + 1) * again.shape[0], :] = again


def momentum_kernel(mom_ref, grad_ref, picks_ref, counts_ref, forward_ref, inverse_ref, out_ref):
    width = mom_ref.shape[1]
    picks = listed(picks_ref[...], counts_ref[...])
    wide = spread_lanes(picks, width, pl.program_id(0) * (width // GROUP))
    forward = forward_ref[...]
    inverse = inverse_ref[...]
    number = numbers()
    moment = 0.9 * mom_ref[...] + grad_ref[...].astype(F32)
    coef = times_right(stack_quads(times_left(forward[:GROUP], moment)), forward)
    kept = []
    for q in range(width // QUAD):
        lanes = wide[:, q * QUAD : (q + 1) * QUAD]
        hit = number == lanes[:1]
        for k in range(1, KMAX):
            hit = hit | (number == lanes[k : k + 1])
        kept.append(jnp.where(hit, coef[q * GROUP : (q + 1) * GROUP], 0.0))
    back = times_right(stack_quads(times_left(inverse[:GROUP], jnp.concatenate(kept, axis=1))), inverse)
    for q in range(width // QUAD):
        cols = slice(q * QUAD, (q + 1) * QUAD)
        out_ref[:, cols] = moment[:, cols] - back[q * GROUP : (q + 1) * GROUP]


def scatter_kernel(got_ref, _, coef_ref, energy_ref, high_ref, low_ref, rows_ref, cols_ref):
    replicas = got_ref.shape[0] // ROWS
    eights = (ROWS - 1) // KMAX
    groups = eights * 8

    def slab(r):
        return got_ref[pl.ds(r, replicas, stride=ROWS), :]

    picks = slab(ROWS - 1)
    picks = jnp.concatenate([picks, picks], axis=0).T
    first = iota((groups, 128), 1) < replicas
    picks = jnp.concatenate([
        jnp.where(first, picks[k * groups : (k + 1) * groups], picks[(k + 1) * groups : (k + 2) * groups])
        for k in range(0, KMAX, 2)
    ], axis=1)
    row_block = jnp.floor(picks * (1.0 / SIDE))
    row_high = jnp.floor(row_block * 0.25)
    rows_ref[...] = row_block - 4.0 * row_high
    cols_ref[...] = row_high * SIDE + (picks - SIDE * row_block)
    for t in range(eights):
        turned = jnp.concatenate([
            jnp.concatenate([slab(t * KMAX + k), slab(t * KMAX + k + 1)], axis=0).T for k in range(0, KMAX, 2)
        ], axis=1)
        high, low = split(turned)
        high_ref[t] = high
        low_ref[t] = low

    upper = iota((8, 128), 0) < BLOCK
    early = iota((8, 128), 1) < GROUP
    block_of_row = iota((GROUP, QUAD), 0).astype(F32)

    def eight(t, energy):
        base = pl.multiple_of(t * 8, 8)
        rows8 = rows_ref[pl.ds(base, 8), :]
        cols8 = cols_ref[pl.ds(base, 8), :]
        for g in range(8):
            vals = [high_ref[t, g * 16 : (g + 1) * 16, :], low_ref[t, g * 16 : (g + 1) * 16, :]]
            row = jnp.broadcast_to(rows8[g : g + 1], (16, QUAD))
            masks = [flag(row == float(b)) for b in range(4)]
            left = jnp.concatenate([m * v for m in masks for v in vals], axis=0)
            onehot = flag(block_of_row == cols8[g : g + 1])
            right = jnp.concatenate([onehot, onehot], axis=0)
            out = lax.dot_general(left, right, (((1,), (1,)), ((), ())), preferred_element_type=F32)
            both = [out[b * 32 : b * 32 + 16] + out[b * 32 + 16 : b * 32 + 32] for b in range(4)]
            for b in range(0, 4, 2):
                for j in range(2):
                    one, two = both[b][j * 8 : j * 8 + 8], both[b + 1][j * 8 : j * 8 + 8]
                    first = jnp.where(upper, one, pltpu.roll(two, BLOCK, 0))
                    second = jnp.where(upper, pltpu.roll(one, BLOCK, 0), two)
                    coef = jnp.where(early, first, second) * (1.0 / replicas)
                    coef_ref[pl.ds(pl.multiple_of(t * 128 + g * 16 + b * 4, 8), 8), j * 128 : (j + 1) * 128] = coef
                    energy = energy + coef * coef
        return energy

    energy = lax.fori_loop(0, eights, eight, jnp.zeros((8, 128), F32), unroll=True)
    energy = jnp.sum(energy, axis=0, keepdims=True)
    energy_ref[...] = jnp.broadcast_to(energy, energy_ref.shape)


def inverse_kernel(core_ref, own_ref, other_ref, weights_ref, update_ref, wide_ref):
    weights = weights_ref[...]
    half_lane = iota((16, 128), 1) < GROUP
    half = update_ref.shape[1] // 2
    mine = core_ref[0] * half
    for coef_ref, start in ((own_ref, mine), (other_ref, half - mine)):
        for t in range(coef_ref.shape[0] // QUAD):
            back = times_right(coef_ref[t * QUAD : (t + 1) * QUAD, :], weights)
            for pair in range(8):
                even = back[pair * 32 : pair * 32 + 16]
                odd = back[pair * 32 + 16 : pair * 32 + 32]
                lanes = slice(pair * 128, (pair + 1) * 128)
                for w in range(2):
                    e = even[:, w * 128 : (w + 1) * 128]
                    o = odd[:, w * 128 : (w + 1) * 128]
                    wide_ref[w * 32 : w * 32 + 16, lanes] = jnp.where(half_lane, e, pltpu.roll(o, GROUP, 1))
                    wide_ref[w * 32 + 16 : w * 32 + 32, lanes] = jnp.where(half_lane, pltpu.roll(e, GROUP, 1), o)
            update_ref[:, pl.ds(pl.multiple_of(start + t * 1024, 1024), 1024)] = times_left(
                weights[:GROUP], wide_ref[...])


def weights_kernel(elements, energy_ref, update_ref, weights_ref, out_hbm, out_ref, sems):
    mean = jnp.broadcast_to(jnp.sum(energy_ref[...]) * (1.0 / elements), (8, 128))
    factor = (0.5 / jnp.sqrt(mean + 1e-06))[:1, :1]
    copies = []
    part = out_ref.shape[0] // 8
    for s in range(8):
        rows = slice(s * part, (s + 1) * part)
        out_ref[rows, :] = weights_ref[rows, :] - update_ref[rows, :] * factor
        copies.append(pltpu.make_async_copy(out_ref.at[rows, :], out_hbm.at[rows, :], sems.at[s]))
        copies[-1].start()
    for copy in copies:
        copy.wait()


def whole(shape):
    return pl.BlockSpec(shape, lambda *_: (0,) * len(shape))


def on_device(momentum, grad, weights, picks, counts):
    width = weights.shape[1]
    nchunk = width // GROUP
    replicas = lax.axis_size("dp")
    nmp = lax.axis_size("mp")
    mat = basis()
    step_width = 1024
    steps = width // step_width
    half = width // 2
    tile = pl.BlockSpec((GROUP, step_width), lambda s: (0, s))
    forward = jnp.asarray(transform_weights(left_weights(mat), right_weights(mat.T)))
    inverse = jnp.asarray(transform_weights(left_weights(mat.T), right_weights(mat)))
    scatter = jnp.asarray(transform_weights(left_weights(mat.T), scatter_weights(mat)))
    hbm = pl.BlockSpec(memory_space=pltpu.HBM)
    vmem = pl.BlockSpec(memory_space=pltpu.VMEM)
    taken = [pltpu.with_memory_space_constraint(x, pltpu.HBM)
             for x in (momentum[0], grad[0], picks[0, 0].T, counts[0], forward)]
    send = pl.pallas_call(
        send_kernel,
        in_specs=[hbm] * 5,
        out_shape=jax.ShapeDtypeStruct((replicas * ROWS, 128), F32),
        scratch_shapes=[
            pltpu.VMEM((GROUP, width), F32),
            pltpu.VMEM((GROUP, width), BF16),
            pltpu.VMEM((KMAX, nchunk), jnp.int32),
            pltpu.VMEM((1, nchunk), jnp.int32),
            pltpu.VMEM(forward.shape, BF16),
            pltpu.SemaphoreType.DMA((5,)),
        ],
        compiler_params=PARAMS,
        name="send",
    )(*taken)

    order = [[(replicas // 2 + 4 + 37 * p) % replicas for p in range(replicas)]]
    got = lax.all_to_all(send.reshape(replicas * ROWS, 1, 128), "dp", 0, 0, tiled=True, axis_index_groups=order)
    new_momentum = pl.pallas_call(
        momentum_kernel,
        grid=(steps,),
        in_specs=[tile, tile, whole((KMAX, nchunk)), whole((1, nchunk)), whole(forward.shape), whole(inverse.shape)],
        out_specs=tile,
        out_shape=jax.ShapeDtypeStruct((GROUP, width), F32),
        compiler_params=PARAMS,
        cost_estimate=pl.CostEstimate(flops=12 * 2 * 2 * GROUP * GROUP * width, bytes_accessed=10 * GROUP * width,
                                      transcendentals=0),
        name="momentum",
    )(*taken, pltpu.with_memory_space_constraint(inverse, pltpu.HBM))
    coef, energy = pl.pallas_call(
        scatter_kernel,
        in_specs=[vmem, hbm],
        out_shape=[jax.ShapeDtypeStruct((half // 4, QUAD), F32), jax.ShapeDtypeStruct((2 * nmp, 128), F32)],
        scratch_shapes=[
            pltpu.VMEM((nchunk // 16, 128, QUAD), BF16),
            pltpu.VMEM((nchunk // 16, 128, QUAD), BF16),
            pltpu.VMEM((nchunk // 2, QUAD), F32),
            pltpu.VMEM((nchunk // 2, QUAD), F32),
        ],
        compiler_params=PARAMS,
        name="scatter",
    )(got.reshape(replicas * ROWS, 128), pltpu.with_memory_space_constraint(new_momentum, pltpu.HBM))
    partners = [[(2 * chip + core) * nmp + z for z in reversed(range(nmp)) for core in range(2)] for chip in range(replicas // 2)]
    energies = lax.all_to_all(energy.reshape(2 * nmp, 1, 128), ("dp", "mp"), 0, 0, tiled=True,
                              axis_index_groups=partners).reshape(2 * nmp, 128)
    other = lax.ppermute(coef, "dp", [(p, p ^ 1) for p in range(replicas)])
    core = jnp.bitwise_and(lax.axis_index("dp"), 1).astype(jnp.int32).reshape(1)
    update = pl.pallas_call(
        inverse_kernel,
        in_specs=[pl.BlockSpec(memory_space=pltpu.SMEM)] + [vmem] * 3,
        out_shape=jax.ShapeDtypeStruct((GROUP, width), F32),
        scratch_shapes=[pltpu.VMEM((GROUP, 1024), F32)],
        compiler_params=PARAMS,
        cost_estimate=pl.CostEstimate(flops=6 * 2 * 2 * GROUP * GROUP * width, bytes_accessed=8 * GROUP * width,
                                      transcendentals=0),
        name="inverse",
    )(core, coef, other, scatter)
    new_weights = pl.pallas_call(
        functools.partial(weights_kernel, float(GROUP * nmp * width)),
        in_specs=[vmem] * 3,
        out_specs=hbm,
        out_shape=jax.ShapeDtypeStruct((GROUP, width), F32),
        scratch_shapes=[pltpu.VMEM((GROUP, width), F32), pltpu.SemaphoreType.DMA((8,))],
        compiler_params=PARAMS,
        name="weights",
    )(energies, update, weights)
    return (new_momentum[None], new_weights)


def solution(mesh):
    in_specs = (
        P("dp", "mp", None),
        P("dp", "mp", None),
        P("mp", None),
        P("dp", "mp", None, None),
        P("dp", "mp", None),
    )
    out_specs = (P("dp", "mp", None), P("mp", None))
    return jax.shard_map(
        on_device, mesh=mesh, in_specs=in_specs, out_specs=out_specs, check_vma=False
    )
```
